768 devices in a mesh: dp: 64 (over y, x, core), seq: 12 (over z).
Axes of the slice: x: 4, y: 8, z: 12, core: 2. Of those that a mesh axis runs over, the one named last changes fastest.
Arguments:
- queries: bfloat16 [12, 12288, 1024], P('seq', 'dp'), may hold values from -6 to 6
- keys: bfloat16 [12, 12288, 1024], P('seq', 'dp'), may hold values from -6 to 6
- values: bfloat16 [12, 12288, 1024], P('seq', 'dp'), may hold values from -6 to 6
- grad_out: bfloat16 [12, 12288, 1024], P('seq', 'dp'), may hold values from -6 to 6
- dest: int32 [12, 12288], P('seq', 'dp'), may hold values from 0 to 12287, as said below
- lengths: int32 [64, 4], P('dp'), may hold values from 1 to 768, 2304 in all within a row
Outputs:
- attended: bfloat16 [12, 12288, 1024], P('seq', 'dp')
- grad_queries: bfloat16 [12, 12288, 1024], P('seq', 'dp')
- grad_keys: bfloat16 [12, 12288, 1024], P('seq', 'dp')
- grad_values: bfloat16 [12, 12288, 1024], P('seq', 'dp')
The draws below stay inside these ranges and needn't reach their ends.
Inputs may be any that keep to these rules, and one draw needn't show every extreme that they name: Each column of dest is a permutation of its 12288 balanced rows; balanced row r belongs to device r // 192; every loader device sends exactly 3 rows to every balanced device of its column. `lengths`: the histories of a pack fill its 2304 rows exactly; in every pack one history has 768 rows.
All inputs are finite; a program needn't handle non-finite values.
Results may differ from the reference program's by a relative error of at most 0.0055.
Values may be sent and summed in bfloat16 or wider, within the bound.
A program may use at most 64 MiB of HBM per device.

```python
import math
import jax
import jax.numpy as jnp
import numpy as np
from jax import lax

HEADS = 8
HDIM = 128
WIDTH = 1024
ROWS = 192
HIST = 4
REACH = 4
MAXLEN = 768
NLOAD = 12288
PACK = 2304
N_DP = 64
N_SEQ = 12


def draw_dest(key, part):
    key = jax.random.fold_in(key, 11)
    first_key, second_key, third_key = jax.random.split(key, 3)
    offsets = jax.vmap(lambda sub: jax.random.permutation(sub, ROWS))(jax.random.split(first_key, N_SEQ)).astype(jnp.int32) % N_DP
    slot_tables = jax.vmap(lambda sub: jax.random.permutation(sub, ROWS))(jax.random.split(second_key, N_SEQ * N_DP)).astype(jnp.int32).reshape(N_SEQ, N_DP, ROWS)
    row_tables = jax.vmap(lambda sub: jax.random.permutation(sub, ROWS))(jax.random.split(third_key, N_SEQ * N_DP)).astype(jnp.int32).reshape(N_SEQ, N_DP, ROWS)
    loader_ids = jnp.arange(N_DP, dtype=jnp.int32)[None, :, None]
    target_dev = (loader_ids + offsets[:, None, :]) % N_DP
    column_ids = jnp.arange(N_SEQ, dtype=jnp.int32)[:, None, None]
    row_ids = jnp.arange(ROWS, dtype=jnp.int32)[None, None, :]
    slot_values = slot_tables[column_ids, target_dev, row_ids]
    targets = target_dev * ROWS + slot_values
    inverse_rows = jnp.argsort(row_tables, axis=-1)
    placed = jnp.take_along_axis(targets, inverse_rows, axis=-1)
    return placed.reshape(N_SEQ, N_DP * ROWS).astype(jnp.int32)


def level_of(key, dims, cuts, smallest, top_value):
    def one(position, parts):
        heights = jax.random.uniform(jax.random.fold_in(jax.random.fold_in(key, 6), position), (parts,), jnp.float32, smallest / len(cuts), top_value / len(cuts))
        return jnp.repeat(jnp.exp(heights), dims[position] // parts).reshape((-1,) + (1,) * (len(dims) - position - 1))

    level = one(*cuts[0])
    for cut in cuts[1:]:
        level = level * one(*cut)
    return level


def profile(amount, total, reach, skew):
    portions = [(1 << 20) // math.isqrt(grade ** skew) + 1 for grade in range(2, amount + 1)]
    rest, holding = total - reach - (amount - 1), [1] * (amount - 1)
    while rest > 0:
        movable = [i for i in range(amount - 1) if holding[i] < reach]
        mass, budget = sum([portions[i] for i in movable]), rest
        for i in movable:
            extra = min(reach - holding[i], max(1, budget * portions[i] // mass), rest)
            holding[i] = holding[i] + extra
            rest = rest - extra
    return np.array([reach] + holding)


def ragged_sizes(own_key, amount, total, reach, lean):
    if amount == 2:
        one = jax.random.randint(own_key, (), max(1, total - reach), min(reach, total - 1) + 1)
        return jnp.stack([one, total - one])
    sizes = jnp.asarray(profile(amount, total, reach, lean), jnp.int32)
    twos = (amount - 1) // 2
    source_of, sink = sizes[1:1 + 2 * twos:2], sizes[2:2 + 2 * twos:2]
    room = jnp.minimum(source_of - 1, reach - sink)
    shifted = jax.random.randint(jax.random.fold_in(own_key, 1), (twos,), 0, 1 << 20) % (room + 1)
    sizes = sizes.at[1:1 + 2 * twos:2].set(source_of - shifted).at[2:2 + 2 * twos:2].set(sink + shifted)
    return sizes[jax.random.permutation(jax.random.fold_in(own_key, 2), amount)]


def gaussian(own_key, extent, scale, limit, cuts=(), held_as=jnp.bfloat16):
    factor_of = level_of(own_key, extent, cuts, -0.22, 0.18) if cuts else 1.0
    values = jax.random.normal(own_key, extent, jnp.float32) * scale * factor_of
    return jnp.minimum(jnp.maximum(values, -limit), limit).astype(held_as)


def setup_inputs(seed: int = 0) -> dict:
    splits = jax.random.split(jax.random.key(seed), 7)
    queries = gaussian(splits[0], (N_SEQ, NLOAD, WIDTH), 1.0, 6.0, ((0, 12), (1, 64)))
    keys = gaussian(splits[1], (N_SEQ, NLOAD, WIDTH), 1.0, 6.0, ((0, 12), (1, 64)))
    values = gaussian(splits[2], (N_SEQ, NLOAD, WIDTH), 1.0, 6.0, ((0, 12), (1, 64)))
    grad_out = gaussian(splits[3], (N_SEQ, NLOAD, WIDTH), 1.0, 6.0, ((0, 12), (1, 64)))
    dest = draw_dest(jax.random.fold_in(splits[6], 71), 0)
    lengths = jax.vmap(lambda own: ragged_sizes(own, HIST, PACK, MAXLEN, 2))(jax.random.split(splits[5], N_DP)).reshape((N_DP, HIST)).astype(jnp.int32)
    return {"queries": queries, "keys": keys, "values": values, "grad_out": grad_out, "dest": dest, "lengths": lengths}


def history_of(rows, history_ends):
    return jnp.sum((rows[..., None] >= history_ends).astype(jnp.int32), axis=-1).astype(jnp.int32)


def block_terms(query, grad, key_part, value_part, weight):
    score_scale = HDIM ** -0.5
    scores = jnp.einsum("bqhd,bkhd->bhqk", query, key_part) * score_scale
    gate_sig = jax.nn.sigmoid(scores)
    weight_heads = weight[:, None]
    mixing = (scores * gate_sig * weight_heads).astype(jnp.bfloat16)
    mixing = lax.optimization_barrier(mixing).astype(jnp.float32)
    outputs = jnp.einsum("bhqk,bkhd->bqhd", mixing, value_part)
    grad_mix = jnp.einsum("bqhd,bkhd->bhqk", grad, value_part)
    grad_score = (grad_mix * weight_heads * gate_sig * (1.0 + scores * (1.0 - gate_sig))).astype(jnp.bfloat16)
    grad_score = lax.optimization_barrier(grad_score).astype(jnp.float32)
    grad_query = jnp.einsum("bhqk,bkhd->bqhd", grad_score, key_part) * score_scale
    grad_key = jnp.einsum("bhqk,bqhd->bkhd", grad_score, query) * score_scale
    grad_value = jnp.einsum("bhqk,bqhd->bkhd", mixing, grad)
    return outputs, grad_query, grad_key, grad_value


def move_blocks(blocks, distance):
    if distance == 0:
        return blocks
    filler = jnp.zeros((distance,) + blocks.shape[1:], blocks.dtype)
    return jnp.concatenate([filler, blocks[:N_SEQ - distance]], axis=0)


def return_blocks(blocks, distance):
    if distance == 0:
        return blocks
    filler = jnp.zeros((distance,) + blocks.shape[1:], blocks.dtype)
    return jnp.concatenate([blocks[distance:], filler], axis=0)


def pack_terms(packed):
    query, key_all, value_all, grad, history_lengths = packed
    query = query.astype(jnp.float32)
    key_all = key_all.astype(jnp.float32)
    value_all = value_all.astype(jnp.float32)
    grad = grad.astype(jnp.float32)
    history_ends = jnp.cumsum(history_lengths).astype(jnp.int32)
    query_rows = (jnp.arange(N_SEQ, dtype=jnp.int32)[:, None] * ROWS + jnp.arange(ROWS, dtype=jnp.int32)[None, :]).astype(jnp.int32)
    query_ids = history_of(query_rows, history_ends)
    row_scale = jnp.full(query_rows.shape, 1.0 / MAXLEN, jnp.float32)
    out_sum = jnp.zeros(query.shape, jnp.float32)
    grad_q_sum = jnp.zeros(query.shape, jnp.float32)
    grad_k_sum = jnp.zeros(query.shape, jnp.float32)
    grad_v_sum = jnp.zeros(query.shape, jnp.float32)
    for distance in range(REACH + 1):
        key_rows = (query_rows - distance * ROWS).astype(jnp.int32)
        key_ids = history_of(key_rows, history_ends)
        mask = (query_ids[:, :, None] == key_ids[:, None, :]) & (key_rows[:, None, :] <= query_rows[:, :, None]) & (key_rows[:, None, :] >= 0)
        weight = jnp.where(mask, row_scale[:, :, None], jnp.float32(0.0))
        outputs, grad_query, grad_key, grad_value = block_terms(query, grad, move_blocks(key_all, distance), move_blocks(value_all, distance), weight)
        out_sum = out_sum + outputs
        grad_q_sum = grad_q_sum + grad_query
        if distance > 0:
            grad_key = lax.optimization_barrier(grad_key.astype(jnp.bfloat16)).astype(jnp.float32)
            grad_value = lax.optimization_barrier(grad_value.astype(jnp.bfloat16)).astype(jnp.float32)
        grad_k_sum = grad_k_sum + return_blocks(grad_key, distance)
        grad_v_sum = grad_v_sum + return_blocks(grad_value, distance)
    return (out_sum.astype(jnp.bfloat16), grad_q_sum.astype(jnp.bfloat16), grad_k_sum.astype(jnp.bfloat16), grad_v_sum.astype(jnp.bfloat16))


def reference(queries, keys, values, grad_out, dest, lengths):
    def to_balanced(loaded):
        placed = jax.vmap(lambda column, targets: jnp.zeros_like(column).at[targets].set(column))(loaded, dest)
        return placed.reshape(N_SEQ, N_DP, ROWS, HEADS, HDIM).transpose(1, 0, 2, 3, 4)

    def to_loader(packed):
        balanced = packed.transpose(1, 0, 2, 3, 4).reshape(N_SEQ, N_DP * ROWS, HEADS * HDIM)
        return jax.vmap(lambda column, targets: column[targets])(balanced, dest)

    results = lax.map(pack_terms, (to_balanced(queries), to_balanced(keys), to_balanced(values), to_balanced(grad_out), lengths))
    return (to_loader(results[0]), to_loader(results[1]), to_loader(results[2]), to_loader(results[3]))
```

```python
import functools

import jax
import jax.numpy as jnp
from jax import lax
from jax.experimental import pallas as pl
from jax.experimental.pallas import tpu as pltpu
from jax.sharding import PartitionSpec as P

HDIM = 128
REACH = 4
MESH = pl.DeviceIdType.MESH


def dot_nt(a, b):
    return lax.dot_general(a, b, (((1,), (1,)), ((), ())), preferred_element_type=jnp.float32)


def dot_tn(a, b):
    return lax.dot_general(a, b, (((0,), (0,)), ((), ())), preferred_element_type=jnp.float32)


def dot_nn(a, b):
    return lax.dot_general(a, b, (((1,), (0,)), ((), ())), preferred_element_type=jnp.float32)


def pair_weight(lengths_ref, query_first, query_count, key_first, key_count):
    shape = (query_count, key_count)
    query_rows = query_first + lax.broadcasted_iota(jnp.int32, shape, 0)
    key_rows = key_first + lax.broadcasted_iota(jnp.int32, shape, 1)
    start = jnp.int32(0)
    first_rows = jnp.zeros(shape, jnp.int32)
    for c in range(lengths_ref.shape[1]):
        start = start + lengths_ref[0, c]
        first_rows = jnp.where(query_rows >= start, start, first_rows)
    mask = (key_rows >= first_rows) & (key_rows <= query_rows)
    return mask


def pair_terms(query, grad, key, value, weight):
    scale = HDIM ** (-0.5)
    scores = dot_nt(query, key) * scale
    sig = 0.5 + 0.5 * jnp.tanh(0.5 * scores)
    mixing = (scores * sig * weight).astype(jnp.bfloat16)
    grad_mix = dot_nt(grad, value)
    grad_score = (grad_mix * weight * sig * (1.0 + scores * (1.0 - sig))).astype(jnp.bfloat16)
    outputs = dot_nn(mixing, value)
    grad_query = dot_nn(grad_score, key) * scale
    grad_key = dot_tn(grad_score, query) * scale
    grad_value = dot_tn(mixing, grad)
    return outputs, grad_query, grad_key, grad_value


def attend_kernel(
    axis,
    lengths_ref,
    slots_ref,
    loaded_ref,
    out_ref,
    keys,
    queries,
    far_out,
    far_in,
    near_out,
    near_in,
    near_sum,
    own_sum,
    weight_own,
    weight_near,
    weight_far,
    in_sems,
    out_sems,
):
    heads = keys.shape[0]
    rows = loaded_ref.shape[1]
    count = lax.axis_size(axis)
    block = lax.axis_index(axis)
    right = {axis: lax.rem(block + 1, count)}
    left = {axis: lax.rem(block + count - 1, count)}

    barrier = pltpu.get_barrier_semaphore()
    for neighbour in (left, right):
        pl.semaphore_signal(barrier, inc=1, device_id=neighbour, device_id_type=MESH)
    pl.semaphore_wait(barrier, 2)

    def copy(src, dst, sems, which, h, target):
        return pltpu.make_async_remote_copy(
            src_ref=src,
            dst_ref=dst,
            send_sem=sems.at[0, which, h],
            recv_sem=sems.at[1, which, h],
            device_id=target,
            device_id_type=MESH,
        )

    def near_copies(h):
        return (
            copy(keys.at[h, :, pl.ds(2 * rows, rows)], keys.at[h, :, pl.ds(rows, rows)], in_sems, 0, h, right),
            copy(queries.at[h, :, pl.ds(0, rows)], queries.at[h, :, pl.ds(rows, rows)], in_sems, 1, h, left),
        )

    def far_copies(h):
        return (
            copy(keys.at[h, :, pl.ds(rows, rows)], keys.at[h, :, pl.ds(0, rows)], in_sems, 2, h, right),
            copy(queries.at[h, :, pl.ds(rows, rows)], queries.at[h, :, pl.ds(2 * rows, rows)], in_sems, 3, h, left),
        )

    def far_returns(h):
        return (
            copy(far_out.at[h, 0], far_in.at[h, 0], out_sems, 0, h, right),
            copy(far_out.at[h, 1], far_in.at[h, 1], out_sems, 1, h, left),
        )

    def near_returns(h):
        return (
            copy(near_out.at[h, 0], near_in.at[h, 0], out_sems, 2, h, right),
            copy(near_out.at[h, 1], near_in.at[h, 1], out_sems, 3, h, left),
        )

    slots = slots_ref[0:1, :]
    place = jnp.where(
        lax.broadcasted_iota(jnp.int32, (rows, rows), 0) == slots, jnp.float32(1.0), jnp.float32(0.0)
    )
    unplace = place.T.astype(jnp.bfloat16)
    place = place.astype(jnp.bfloat16)
    for pair in range(heads // 2):
        lanes = pl.ds(pair * 2 * HDIM, 2 * HDIM)
        for a, (buffer, k, start) in enumerate(
            ((queries, 0, 0), (keys, 0, 2 * rows), (keys, 1, 2 * rows), (queries, 1, 0))
        ):
            placed = dot_nn(place, loaded_ref[a, :, lanes]).astype(jnp.bfloat16)
            buffer[2 * pair, k, pl.ds(start, rows), :] = placed[:, :HDIM]
            buffer[2 * pair + 1, k, pl.ds(start, rows), :] = placed[:, HDIM:]
        for h in (2 * pair, 2 * pair + 1):
            for c in near_copies(h):
                c.start()

    weight = jnp.float32(1.0 / (REACH * rows))
    first = block * rows
    for ref, query_first, key_first in (
        (weight_own, first, first - rows),
        (weight_near, first + rows, first - 2 * rows),
        (weight_far, first + 2 * rows, first - 2 * rows),
    ):
        mask = pair_weight(lengths_ref, query_first, ref.shape[0], key_first, ref.shape[1])
        ref[...] = jnp.where(mask, weight, jnp.float32(0.0))

    def forward(h, carry):
        for c in near_copies(h):
            c.wait_recv()
        for c in far_copies(h):
            c.start()
        return carry

    lax.fori_loop(0, heads, forward, 0)

    def compute(h, carry):
        for c in far_copies(h):
            c.wait_recv()
        key, value = keys[h, 0], keys[h, 1]
        query, grad = queries[h, 0], queries[h, 1]
        far = pair_terms(query[2 * rows :], grad[2 * rows :], key[:rows], value[:rows], weight_far[...])
        near = pair_terms(
            query[rows : 2 * rows], grad[rows : 2 * rows], key[: 2 * rows], value[: 2 * rows], weight_near[...]
        )
        far_out[h, 0, 0] = far[0].astype(jnp.bfloat16)
        far_out[h, 0, 1] = far[1].astype(jnp.bfloat16)
        far_out[h, 1, 0] = (far[2] + near[2][:rows]).astype(jnp.bfloat16)
        far_out[h, 1, 1] = (far[3] + near[3][:rows]).astype(jnp.bfloat16)
        for c in far_returns(h):
            c.start()
        own = pair_terms(query[:rows], grad[:rows], key[rows:], value[rows:], weight_own[...])
        near_sum[h, 0, 0] = near[0]
        near_sum[h, 0, 1] = near[1]
        near_sum[h, 1, 0] = near[2][rows:] + own[2][:rows]
        near_sum[h, 1, 1] = near[3][rows:] + own[3][:rows]
        own_sum[h, 0, 0] = own[0]
        own_sum[h, 0, 1] = own[1]
        own_sum[h, 1, 0] = own[2][rows:]
        own_sum[h, 1, 1] = own[3][rows:]
        return carry

    lax.fori_loop(0, heads, compute, 0)

    def relay(h, carry):
        for c in far_returns(h):
            c.wait_recv()
        near_out[h] = (near_sum[h] + far_in[h].astype(jnp.float32)).astype(jnp.bfloat16)
        for c in near_returns(h):
            c.start()
        return carry

    lax.fori_loop(0, heads, relay, 0)

    def finish(h, carry):
        for c in near_returns(h):
            c.wait_recv()
        lanes = pl.ds(pl.multiple_of(h * HDIM, HDIM), HDIM)
        for side in range(2):
            for k in range(2):
                total = (own_sum[h, side, k] + near_in[h, side, k].astype(jnp.float32)).astype(jnp.bfloat16)
                out_ref[2 * side + k, :, lanes] = dot_nn(unplace, total).astype(jnp.bfloat16)
        for c in near_copies(h) + far_copies(h) + far_returns(h) + near_returns(h):
            c.wait_send()
        return carry

    lax.fori_loop(0, heads, finish, 0)


def attend(loaded, slots, lengths):
    _, rows, width = loaded.shape
    heads = width // HDIM
    blocks = lambda *lead: pltpu.VMEM((heads,) + lead + (HDIM,), jnp.bfloat16)
    totals = pltpu.VMEM((heads, 2, 2, rows, HDIM), jnp.float32)
    return pl.pallas_call(
        functools.partial(attend_kernel, "seq"),
        out_shape=jax.ShapeDtypeStruct(loaded.shape, jnp.bfloat16),
        in_specs=[
            pl.BlockSpec(memory_space=pltpu.SMEM),
            pl.BlockSpec(memory_space=pltpu.VMEM),
            pl.BlockSpec(memory_space=pltpu.VMEM),
        ],
        out_specs=pl.BlockSpec(memory_space=pltpu.VMEM),
        scratch_shapes=[
            blocks(2, 3 * rows),
            blocks(2, 3 * rows),
            blocks(2, 2, rows),
            blocks(2, 2, rows),
            blocks(2, 2, rows),
            blocks(2, 2, rows),
            totals,
            totals,
            pltpu.VMEM((rows, 2 * rows), jnp.float32),
            pltpu.VMEM((rows, 2 * rows), jnp.float32),
            pltpu.VMEM((rows, rows), jnp.float32),
            pltpu.SemaphoreType.DMA((2, 4, heads)),
            pltpu.SemaphoreType.DMA((2, 4, heads)),
        ],
        compiler_params=pltpu.CompilerParams(
            collective_id=0, has_side_effects=True, vmem_limit_bytes=48 * 1024 * 1024
        ),
        name="attend",
    )(lengths, slots, loaded)


def shards(queries, keys, values, grad_out, dest, lengths):
    row_count = queries.shape[1]
    width = queries.shape[2]
    peer_count = lax.axis_size("dp")
    per_peer = row_count // peer_count
    targets = dest[0]
    send_order = jnp.argsort(targets)
    slot_out = (targets[send_order] % row_count).reshape(1, peer_count, per_peer)
    packet = jnp.stack([queries[0], keys[0], values[0], grad_out[0]])[:, send_order].reshape(
        4, peer_count, per_peer, width
    )
    packet_in, slot_in = (
        lax.all_to_all(packet, "dp", split_axis=1, concat_axis=1, tiled=True),
        lax.all_to_all(slot_out, "dp", split_axis=1, concat_axis=1, tiled=True),
    )
    slots = jnp.broadcast_to(slot_in.reshape(1, row_count), (8, row_count))
    outgoing = attend(packet_in.reshape(4, row_count, width), slots, lengths).reshape(
        4, peer_count, per_peer, width
    )
    returned = lax.all_to_all(outgoing, "dp", split_axis=1, concat_axis=1, tiled=True).reshape(
        4, row_count, width
    )
    restored = returned[:, jnp.argsort(send_order)]
    return (restored[0][None], restored[1][None], restored[2][None], restored[3][None])


def solution(mesh):
    rows = P("seq", "dp", None)
    return jax.shard_map(
        shards,
        mesh=mesh,
        in_specs=(rows, rows, rows, rows, P("seq", "dp"), P("dp", None)),
        out_specs=(rows, rows, rows, rows),
        check_vma=False,
    )
```

```python
import functools

import jax
import jax.numpy as jnp
from jax import lax
from jax.experimental import pallas as pl
from jax.experimental.pallas import tpu as pltpu
from jax.sharding import PartitionSpec as P

HDIM = 128
REACH = 4
MESH = pl.DeviceIdType.MESH


def dot_nt(a, b):
    return lax.dot_general(a, b, (((1,), (1,)), ((), ())), preferred_element_type=jnp.float32)


def dot_tn(a, b):
    return lax.dot_general(a, b, (((0,), (0,)), ((), ())), preferred_element_type=jnp.float32)


def dot_nn(a, b):
    return lax.dot_general(a, b, (((1,), (0,)), ((), ())), preferred_element_type=jnp.float32)


def pair_weight(lengths_ref, query_first, query_count, key_first, key_count):
    shape = (query_count, key_count)
    query_rows = query_first + lax.broadcasted_iota(jnp.int32, shape, 0)
    key_rows = key_first + lax.broadcasted_iota(jnp.int32, shape, 1)
    start = jnp.int32(0)
    first_rows = jnp.zeros(shape, jnp.int32)
    for c in range(lengths_ref.shape[1]):
        start = start + lengths_ref[0, c]
        first_rows = jnp.where(query_rows >= start, start, first_rows)
    mask = (key_rows >= first_rows) & (key_rows <= query_rows)
    return mask


def pair_terms(query, grad, key, value, weight):
    scale = HDIM ** (-0.5)
    scores = dot_nt(query, key) * scale
    sig = 0.5 + 0.5 * jnp.tanh(0.5 * scores)
    mixing = (scores * sig * weight).astype(jnp.bfloat16)
    grad_mix = dot_nt(grad, value)
    grad_score = (grad_mix * weight * sig * (1.0 + scores * (1.0 - sig))).astype(jnp.bfloat16)
    outputs = dot_nn(mixing, value)
    grad_query = dot_nn(grad_score, key) * scale
    grad_key = dot_tn(grad_score, query) * scale
    grad_value = dot_tn(mixing, grad)
    return outputs, grad_query, grad_key, grad_value


def whole_kernel(
    lengths_ref,
    dest_ref,
    query_ref,
    key_ref,
    value_ref,
    grad_ref,
    out_ref,
    grad_query_ref,
    grad_key_ref,
    grad_value_ref,
    mixed,
    packed,
    arrived,
    packed_back,
    arrived_back,
    slots_out,
    slots_in,
    keys,
    queries,
    far_out,
    far_in,
    near_out,
    near_in,
    near_sum,
    own_sum,
    weight_own,
    weight_near,
    weight_far,
    in_sems,
    out_sems,
    all_sems,
):
    heads = keys.shape[0]
    half_heads = heads // 2
    chunks = 4 * half_heads
    rows = query_ref.shape[0]
    peers = lax.axis_size("dp")
    per_peer = rows // peers
    part = per_peer * chunks
    me = lax.axis_index("dp")
    count = lax.axis_size("seq")
    block = lax.axis_index("seq")
    right = {"seq": lax.rem(block + 1, count)}
    left = {"seq": lax.rem(block + count - 1, count)}

    def peer_at(i):
        return lax.rem(me + lax.rem(i * 37, peers), peers)

    barrier = pltpu.get_barrier_semaphore()
    for neighbour in (left, right):
        pl.semaphore_signal(barrier, inc=1, device_id=neighbour, device_id_type=MESH)

    def greet(i, carry):
        pl.semaphore_signal(barrier, inc=1, device_id={"dp": peer_at(i)}, device_id_type=MESH)
        return carry

    lax.fori_loop(1, peers, greet, 0)

    def copy(src, dst, sems, which, h, target):
        return pltpu.make_async_remote_copy(
            src_ref=src,
            dst_ref=dst,
            send_sem=sems.at[0, which, h],
            recv_sem=sems.at[1, which, h],
            device_id=target,
            device_id_type=MESH,
        )

    def near_copies(h):
        return (
            copy(keys.at[h, :, pl.ds(2 * rows, rows)], keys.at[h, :, pl.ds(rows, rows)], in_sems, 0, h, right),
            copy(queries.at[h, :, pl.ds(0, rows)], queries.at[h, :, pl.ds(rows, rows)], in_sems, 1, h, left),
        )

    def far_copies(h):
        return (
            copy(keys.at[h, :, pl.ds(rows, rows)], keys.at[h, :, pl.ds(0, rows)], in_sems, 2, h, right),
            copy(queries.at[h, :, pl.ds(rows, rows)], queries.at[h, :, pl.ds(2 * rows, rows)], in_sems, 3, h, left),
        )

    def far_returns(h):
        return (
            copy(far_out.at[h, 0], far_in.at[h, 0], out_sems, 0, h, right),
            copy(far_out.at[h, 1], far_in.at[h, 1], out_sems, 1, h, left),
        )

    def near_returns(h):
        return (
            copy(near_out.at[h, 0], near_in.at[h, 0], out_sems, 2, h, right),
            copy(near_out.at[h, 1], near_in.at[h, 1], out_sems, 3, h, left),
        )

    def send_half(source, target, half, which):
        def send(i, carry):
            peer = peer_at(i)
            source[half, peer] = mixed[pl.ds(pl.multiple_of(peer * part, 16), part), :].astype(jnp.bfloat16)
            copy(source.at[half, peer], target.at[half, me], all_sems, which, half, {"dp": peer}).start()
            return carry

        lax.fori_loop(1, peers, send, 0)
        target[half, me] = mixed[pl.ds(pl.multiple_of(me * part, 16), part), :].astype(jnp.bfloat16)

    def wait_all(ref, side, which, half):
        whole = ref.at[half, pl.ds(0, peers - 1)]
        pltpu.make_async_copy(whole, whole, all_sems.at[side, which, half]).wait()

    def spread(source, half):
        mixed[...] = source[half].reshape(peers * part, HDIM).astype(jnp.float32)

    targets = dest_ref[...].astype(jnp.float32)
    across = jnp.broadcast_to(targets, (rows, rows))
    ranks = jnp.sum(jnp.where(across.T < across, jnp.float32(1.0), jnp.float32(0.0)), axis=0, keepdims=True)
    steps = lax.broadcasted_iota(jnp.int32, (rows, rows), 0).astype(jnp.float32)
    order = jnp.where(steps == ranks, jnp.float32(1.0), jnp.float32(0.0))
    restore = order.T.astype(jnp.bfloat16)
    order = order.astype(jnp.bfloat16)

    def pack_half(half):
        for a, ref in enumerate((query_ref, key_ref, value_ref, grad_ref)):
            for pair in range(half_heads // 2):
                lanes = pl.ds((half * half_heads + 2 * pair) * HDIM, 2 * HDIM)
                sorted_rows = dot_nn(order, ref[:, lanes])
                mixed[pl.ds(8 * pair + a, rows, stride=chunks), :] = sorted_rows[:, :HDIM]
                mixed[pl.ds(8 * pair + 4 + a, rows, stride=chunks), :] = sorted_rows[:, HDIM:]

    pack_half(0)
    pl.semaphore_wait(barrier, peers + 1)
    send_half(packed, arrived, 0, 0)

    width = slots_out.shape[2]
    lane = lax.broadcasted_iota(jnp.int32, (peers, 1, width), 2)
    slots = jnp.zeros((peers, 1, width), jnp.float32)
    first_rank = (lax.broadcasted_iota(jnp.int32, (peers, 1, rows), 0) * per_peer).astype(jnp.float32)
    base = (lax.broadcasted_iota(jnp.int32, (peers, 1, 1), 0) * rows).astype(jnp.float32)
    for t in range(per_peer):
        hit = ranks.reshape(1, 1, rows) == first_rank + t
        slot = jnp.sum(jnp.where(hit, targets.reshape(1, 1, rows), jnp.float32(0.0)), axis=2, keepdims=True) - base
        slots = jnp.where(lane == me * per_peer + t, slot, slots)
    slots_out[...] = slots

    def send_slots(i, carry):
        peer = peer_at(i)
        copy(slots_out.at[peer], slots_in.at[me], all_sems, 2, 0, {"dp": peer}).start()
        return carry

    lax.fori_loop(1, peers, send_slots, 0)
    slots_in[me] = slots_out[me]

    pack_half(1)
    send_half(packed, arrived, 1, 0)

    weight = jnp.float32(1.0 / (REACH * rows))
    first = block * rows
    for ref, query_first, key_first in (
        (weight_own, first, first - rows),
        (weight_near, first + rows, first - 2 * rows),
        (weight_far, first + 2 * rows, first - 2 * rows),
    ):
        mask = pair_weight(lengths_ref, query_first, ref.shape[0], key_first, ref.shape[1])
        ref[...] = jnp.where(mask, weight, jnp.float32(0.0))

    everyone = slots_in.at[pl.ds(0, peers - 1)]
    pltpu.make_async_copy(everyone, everyone, all_sems.at[1, 2, 0]).wait()
    slot_row = jnp.sum(slots_in[...], axis=0)[:, :rows]
    place = jnp.where(steps == slot_row, jnp.float32(1.0), jnp.float32(0.0))
    unplace = place.T.astype(jnp.bfloat16)
    place = place.astype(jnp.bfloat16)

    def place_half(half):
        wait_all(arrived, 1, 0, half)
        spread(arrived, half)
        for i in range(half_heads):
            h = half * half_heads + i
            for a, (buffer, k, start) in enumerate(
                ((queries, 0, 0), (keys, 0, 2 * rows), (keys, 1, 2 * rows), (queries, 1, 0))
            ):
                came = mixed[pl.ds(4 * i + a, rows, stride=chunks), :].astype(jnp.bfloat16)
                buffer[h, k, pl.ds(start, rows), :] = dot_nn(place, came).astype(jnp.bfloat16)
            for c in near_copies(h):
                c.start()

    def each_head(half, step):
        def run(h, carry):
            step(h)
            return carry

        lax.fori_loop(half * half_heads, (half + 1) * half_heads, run, 0)

    def forward(h):
        for c in near_copies(h):
            c.wait_recv()
        for c in far_copies(h):
            c.start()

    def compute(h):
        for c in far_copies(h):
            c.wait_recv()
        key, value = keys[h, 0], keys[h, 1]
        query, grad = queries[h, 0], queries[h, 1]
        far = pair_terms(query[2 * rows :], grad[2 * rows :], key[:rows], value[:rows], weight_far[...])
        near = pair_terms(
            query[rows : 2 * rows], grad[rows : 2 * rows], key[: 2 * rows], value[: 2 * rows], weight_near[...]
        )
        far_out[h, 0, 0] = far[0].astype(jnp.bfloat16)
        far_out[h, 0, 1] = far[1].astype(jnp.bfloat16)
        far_out[h, 1, 0] = (far[2] + near[2][:rows]).astype(jnp.bfloat16)
        far_out[h, 1, 1] = (far[3] + near[3][:rows]).astype(jnp.bfloat16)
        for c in far_returns(h):
            c.start()
        own = pair_terms(query[:rows], grad[:rows], key[rows:], value[rows:], weight_own[...])
        near_sum[h, 0, 0] = near[0]
        near_sum[h, 0, 1] = near[1]
        near_sum[h, 1, 0] = near[2][rows:] + own[2][:rows]
        near_sum[h, 1, 1] = near[3][rows:] + own[3][:rows]
        own_sum[h, 0, 0] = own[0]
        own_sum[h, 0, 1] = own[1]
        own_sum[h, 1, 0] = own[2][rows:]
        own_sum[h, 1, 1] = own[3][rows:]

    def relay(h):
        for c in far_returns(h):
            c.wait_recv()
        near_out[h] = (near_sum[h] + far_in[h].astype(jnp.float32)).astype(jnp.bfloat16)
        for c in near_returns(h):
            c.start()

    def finish_half(half):
        for i in range(half_heads):
            h = half * half_heads + i
            for c in near_returns(h):
                c.wait_recv()
            for side in range(2):
                for k in range(2):
                    total = (own_sum[h, side, k] + near_in[h, side, k].astype(jnp.float32)).astype(jnp.bfloat16)
                    mixed[pl.ds(4 * i + 2 * side + k, rows, stride=chunks), :] = dot_nn(unplace, total)
        send_half(packed_back, arrived_back, half, 1)

    def restore_half(half):
        wait_all(arrived_back, 1, 1, half)
        spread(arrived_back, half)
        for i in range(half_heads):
            lanes = pl.ds((half * half_heads + i) * HDIM, HDIM)
            for a, ref in enumerate((out_ref, grad_query_ref, grad_key_ref, grad_value_ref)):
                came = mixed[pl.ds(4 * i + a, rows, stride=chunks), :].astype(jnp.bfloat16)
                ref[:, lanes] = dot_nn(restore, came).astype(jnp.bfloat16)

    place_half(0)
    each_head(0, forward)
    each_head(0, compute)
    place_half(1)
    each_head(0, relay)
    each_head(1, forward)
    finish_half(0)
    each_head(1, compute)
    each_head(1, relay)
    restore_half(0)
    finish_half(1)

    def settle(h):
        for c in near_copies(h) + far_copies(h) + far_returns(h) + near_returns(h):
            c.wait_send()

    each_head(0, settle)
    each_head(1, settle)
    for half in range(2):
        wait_all(packed, 0, 0, half)
        wait_all(packed_back, 0, 1, half)
    pltpu.make_async_copy(everyone, everyone, all_sems.at[0, 2, 0]).wait()
    restore_half(1)


def shards(queries, keys, values, grad_out, dest, lengths):
    _, rows, width = queries.shape
    heads = width // HDIM
    peers = lax.axis_size("dp")
    part = rows // peers * 2 * heads
    blocks = lambda *lead: pltpu.VMEM((heads,) + lead + (HDIM,), jnp.bfloat16)
    totals = pltpu.VMEM((heads, 2, 2, rows, HDIM), jnp.float32)
    halves = pltpu.VMEM((2, peers, part, HDIM), jnp.bfloat16)
    slots = pltpu.VMEM((peers, 1, (rows + 127) // 128 * 128), jnp.float32)
    vmem = pl.BlockSpec(memory_space=pltpu.VMEM)
    results = pl.pallas_call(
        whole_kernel,
        out_shape=[jax.ShapeDtypeStruct((rows, width), jnp.bfloat16)] * 4,
        in_specs=[pl.BlockSpec(memory_space=pltpu.SMEM)] + [vmem] * 5,
        out_specs=[vmem] * 4,
        scratch_shapes=[
            pltpu.VMEM((peers * part, HDIM), jnp.float32),
            halves,
            halves,
            halves,
            halves,
            slots,
            slots,
            blocks(2, 3 * rows),
            blocks(2, 3 * rows),
            blocks(2, 2, rows),
            blocks(2, 2, rows),
            blocks(2, 2, rows),
            blocks(2, 2, rows),
            totals,
            totals,
            pltpu.VMEM((rows, 2 * rows), jnp.float32),
            pltpu.VMEM((rows, 2 * rows), jnp.float32),
            pltpu.VMEM((rows, rows), jnp.float32),
            pltpu.SemaphoreType.DMA((2, 4, heads)),
            pltpu.SemaphoreType.DMA((2, 4, heads)),
            pltpu.SemaphoreType.DMA((2, 3, 2)),
        ],
        compiler_params=pltpu.CompilerParams(
            collective_id=0, has_side_effects=True, vmem_limit_bytes=52 * 1024 * 1024
        ),
        name="whole",
    )(lengths, dest, queries[0], keys[0], values[0], grad_out[0])
    return tuple(result[None] for result in results)


def solution(mesh):
    rows = P("seq", "dp", None)
    return jax.shard_map(
        shards,
        mesh=mesh,
        in_specs=(rows, rows, rows, rows, P("seq", "dp"), P("dp", None)),
        out_specs=(rows, rows, rows, rows),
        check_vma=False,
    )
```

```python
import functools

import jax
import jax.numpy as jnp
from jax import lax
from jax.experimental import pallas as pl
from jax.experimental.pallas import tpu as pltpu
from jax.sharding import PartitionSpec as P

HDIM = 128
REACH = 4
GROUPS = 4
MESH = pl.DeviceIdType.MESH


def dot_nt(a, b):
    return lax.dot_general(a, b, (((1,), (1,)), ((), ())), preferred_element_type=jnp.float32)


def dot_tn(a, b):
    return lax.dot_general(a, b, (((0,), (0,)), ((), ())), preferred_element_type=jnp.float32)


def dot_nn(a, b):
    return lax.dot_general(a, b, (((1,), (0,)), ((), ())), preferred_element_type=jnp.float32)


def pair_weight(lengths_ref, query_first, query_count, key_first, key_count):
    shape = (query_count, key_count)
    query_rows = query_first + lax.broadcasted_iota(jnp.int32, shape, 0)
    key_rows = key_first + lax.broadcasted_iota(jnp.int32, shape, 1)
    start = jnp.int32(0)
    first_rows = jnp.zeros(shape, jnp.int32)
    for c in range(lengths_ref.shape[1]):
        start = start + lengths_ref[0, c]
        first_rows = jnp.where(query_rows >= start, start, first_rows)
    mask = (key_rows >= first_rows) & (key_rows <= query_rows)
    return mask


def pair_terms(query, grad, key, value, weight):
    scale = HDIM ** (-0.5)
    scores = dot_nt(query, key) * scale
    sig = 0.5 + 0.5 * jnp.tanh(0.5 * scores)
    mixing = (scores * sig * weight).astype(jnp.bfloat16)
    grad_mix = dot_nt(grad, value)
    grad_score = (grad_mix * weight * sig * (1.0 + scores * (1.0 - sig))).astype(jnp.bfloat16)
    outputs = dot_nn(mixing, value)
    grad_query = dot_nn(grad_score, key) * scale
    grad_key = dot_tn(grad_score, query) * scale
    grad_value = dot_tn(mixing, grad)
    return outputs, grad_query, grad_key, grad_value


def whole_kernel(
    lengths_ref,
    dest_ref,
    query_ref,
    key_ref,
    value_ref,
    grad_ref,
    out_ref,
    grad_query_ref,
    grad_key_ref,
    grad_value_ref,
    mixed,
    packed,
    arrived,
    packed_back,
    arrived_back,
    handed,
    came,
    handed_back,
    came_back,
    slots_out,
    slots_in,
    keys,
    queries,
    far_out,
    far_in,
    near_out,
    near_in,
    near_sum,
    own_sum,
    weight_own,
    weight_near,
    weight_far,
    in_sems,
    out_sems,
    all_sems,
):
    heads = keys.shape[0]
    group_heads = heads // GROUPS
    chunks = 4 * group_heads
    rows = query_ref.shape[0]
    peers = lax.axis_size("dp")
    chips = peers // 2
    per_peer = rows // peers
    part = 2 * per_peer * chunks
    shared = per_peer * chips
    me = lax.axis_index("dp")
    chip = me // 2
    core = lax.rem(me, 2)
    sibling = {"dp": 2 * chip + 1 - core}
    count = lax.axis_size("seq")
    block = lax.axis_index("seq")
    right = {"seq": lax.rem(block + 1, count)}
    left = {"seq": lax.rem(block + count - 1, count)}

    barrier = pltpu.get_barrier_semaphore()
    for neighbour in (left, right):
        pl.semaphore_signal(barrier, inc=1, device_id=neighbour, device_id_type=MESH)

    def greet(i, carry):
        pl.semaphore_signal(barrier, inc=1, device_id={"dp": lax.rem(me + i, peers)}, device_id_type=MESH)
        return carry

    lax.fori_loop(1, peers, greet, 0)

    def copy(src, dst, sems, which, h, target):
        return pltpu.make_async_remote_copy(
            src_ref=src,
            dst_ref=dst,
            send_sem=sems.at[0, which, h],
            recv_sem=sems.at[1, which, h],
            device_id=target,
            device_id_type=MESH,
        )

    def near_copies(h):
        return (
            copy(keys.at[h, :, pl.ds(2 * rows, rows)], keys.at[h, :, pl.ds(rows, rows)], in_sems, 0, h, right),
            copy(queries.at[h, :, pl.ds(0, rows)], queries.at[h, :, pl.ds(rows, rows)], in_sems, 1, h, left),
        )

    def far_copies(h):
        return (
            copy(keys.at[h, :, pl.ds(rows, rows)], keys.at[h, :, pl.ds(0, rows)], in_sems, 2, h, right),
            copy(queries.at[h, :, pl.ds(rows, rows)], queries.at[h, :, pl.ds(2 * rows, rows)], in_sems, 3, h, left),
        )

    def far_returns(h):
        return (
            copy(far_out.at[h, 0], far_in.at[h, 0], out_sems, 0, h, right),
            copy(far_out.at[h, 1], far_in.at[h, 1], out_sems, 1, h, left),
        )

    def near_returns(h):
        return (
            copy(near_out.at[h, 0], near_in.at[h, 0], out_sems, 2, h, right),
            copy(near_out.at[h, 1], near_in.at[h, 1], out_sems, 3, h, left),
        )

    def send_group(source, target, g, which):
        def send(i, carry):
            other = lax.rem(chip + i, chips)
            source[g, other] = mixed[pl.ds(pl.multiple_of(other * part, 16), part), :].astype(jnp.bfloat16)
            copy(source.at[g, other], target.at[g, chip], all_sems, which, g, {"dp": 2 * other + core}).start()
            return carry

        lax.fori_loop(1, chips, send, 0)
        target[g, chip] = mixed[pl.ds(pl.multiple_of(chip * part, 16), part), :].astype(jnp.bfloat16)

    def wait_all(ref, side, which, g):
        whole = ref.at[g, pl.ds(0, chips - 1)]
        pltpu.make_async_copy(whole, whole, all_sems.at[side, which, g]).wait()

    def hand_copy(source, target, g, which):
        return copy(source.at[g], target.at[g, :, pl.ds(shared, shared)], all_sems, which, g, sibling)

    def hand_over(source, given, target, g, which):
        wait_all(source, 1, which, g)
        mixed[...] = source[g].reshape(chips * part, HDIM).astype(jnp.float32)
        for c in range(chunks):
            for t in range(per_peer):
                first = mixed[pl.ds(t * chunks + c, chips, stride=part), :]
                second = mixed[pl.ds((per_peer + t) * chunks + c, chips, stride=part), :]
                target[g, c, pl.ds(t * chips, chips), :] = jnp.where(core == 0, first, second).astype(jnp.bfloat16)
                given[g, c, pl.ds(t * chips, chips), :] = jnp.where(core == 0, second, first).astype(jnp.bfloat16)
        hand_copy(given, target, g, which + 3).start()

    targets = dest_ref[...].astype(jnp.float32)
    across = jnp.broadcast_to(targets, (rows, rows))
    ranks = jnp.sum(jnp.where(across.T < across, jnp.float32(1.0), jnp.float32(0.0)), axis=0, keepdims=True)
    steps = lax.broadcasted_iota(jnp.int32, (rows, rows), 0).astype(jnp.float32)
    order = jnp.where(steps == ranks, jnp.float32(1.0), jnp.float32(0.0)).astype(jnp.bfloat16)
    holder = jnp.floor((ranks + 0.5) * (1.0 / per_peer))
    holder_chip = jnp.floor((holder + 0.5) * 0.5)
    away = jnp.abs(holder - 2.0 * holder_chip - core.astype(jnp.float32))
    spots = away * shared + (ranks - holder * per_peer) * chips + holder_chip
    restore = jnp.where(steps == spots, jnp.float32(1.0), jnp.float32(0.0)).T.astype(jnp.bfloat16)

    def pack_group(g):
        for a, ref in enumerate((query_ref, key_ref, value_ref, grad_ref)):
            sorted_rows = dot_nn(order, ref[:, pl.ds(g * group_heads * HDIM, group_heads * HDIM)])
            for i in range(group_heads):
                mixed[pl.ds(4 * i + a, rows, stride=chunks), :] = sorted_rows[:, i * HDIM : (i + 1) * HDIM]
        send_group(packed, arrived, g, 0)

    pl.semaphore_wait(barrier, peers + 1)
    pack_group(0)

    width = slots_out.shape[2]
    lane = lax.broadcasted_iota(jnp.int32, (peers, 1, width), 2)
    receiver = lax.broadcasted_iota(jnp.int32, (peers, 1, 1), 0)
    apart = jnp.where(lax.rem(receiver, 2) == core, 0, shared)
    slots = jnp.zeros((peers, 1, width), jnp.float32)
    base = (receiver * rows).astype(jnp.float32)
    first_rank = (receiver * per_peer).astype(jnp.float32)
    for t in range(per_peer):
        hit = ranks.reshape(1, 1, rows) == first_rank + t
        slot = jnp.sum(jnp.where(hit, targets.reshape(1, 1, rows), jnp.float32(0.0)), axis=2, keepdims=True) - base
        slots = jnp.where(lane == apart + t * chips + chip, slot, slots)
        slots = jnp.where(lane == width // 2 + me * per_peer + t, slot, slots)
    slots_out[...] = slots

    def send_slots(i, carry):
        peer = lax.rem(me + i, peers)
        copy(slots_out.at[peer], slots_in.at[me], all_sems, 2, 0, {"dp": peer}).start()
        return carry

    lax.fori_loop(1, peers, send_slots, 0)
    slots_in[me] = slots_out[me]

    for g in range(1, GROUPS):
        pack_group(g)

    weight = jnp.float32(1.0 / (REACH * rows))
    first = block * rows
    for ref, query_first, key_first in (
        (weight_own, first, first - rows),
        (weight_near, first + rows, first - 2 * rows),
        (weight_far, first + 2 * rows, first - 2 * rows),
    ):
        mask = pair_weight(lengths_ref, query_first, ref.shape[0], key_first, ref.shape[1])
        ref[...] = jnp.where(mask, weight, jnp.float32(0.0))

    everyone = slots_in.at[pl.ds(0, peers - 1)]
    pltpu.make_async_copy(everyone, everyone, all_sems.at[1, 2, 0]).wait()
    slot_row = jnp.sum(slots_in[...], axis=0)
    place = jnp.where(steps == slot_row[:, :rows], jnp.float32(1.0), jnp.float32(0.0)).astype(jnp.bfloat16)
    back = slot_row[:, width // 2 : width // 2 + rows]
    unplace = jnp.where(steps == back, jnp.float32(1.0), jnp.float32(0.0)).T.astype(jnp.bfloat16)

    def each_head(g, step):
        def run(h, carry):
            step(h)
            return carry

        lax.fori_loop(g * group_heads, (g + 1) * group_heads, run, 0)

    def unpack(g):
        hand_over(arrived, handed, came, g, 0)

    def place_group(g):
        hand_copy(handed, came, g, 3).wait_recv()
        for i in range(group_heads):
            h = g * group_heads + i
            for a, (buffer, k, start) in enumerate(
                ((queries, 0, 0), (keys, 0, 2 * rows), (keys, 1, 2 * rows), (queries, 1, 0))
            ):
                buffer[h, k, pl.ds(start, rows), :] = dot_nn(place, came[g, 4 * i + a]).astype(jnp.bfloat16)
            for c in near_copies(h):
                c.start()

    def forward(h):
        for c in near_copies(h):
            c.wait_recv()
        for c in far_copies(h):
            c.start()

    def compute(h):
        for c in far_copies(h):
            c.wait_recv()
        key, value = keys[h, 0], keys[h, 1]
        query, grad = queries[h, 0], queries[h, 1]
        far = pair_terms(query[2 * rows :], grad[2 * rows :], key[:rows], value[:rows], weight_far[...])
        near = pair_terms(
            query[rows : 2 * rows], grad[rows : 2 * rows], key[: 2 * rows], value[: 2 * rows], weight_near[...]
        )
        far_out[h, 0, 0] = far[0].astype(jnp.bfloat16)
        far_out[h, 0, 1] = far[1].astype(jnp.bfloat16)
        far_out[h, 1, 0] = (far[2] + near[2][:rows]).astype(jnp.bfloat16)
        far_out[h, 1, 1] = (far[3] + near[3][:rows]).astype(jnp.bfloat16)
        for c in far_returns(h):
            c.start()
        own = pair_terms(query[:rows], grad[:rows], key[rows:], value[rows:], weight_own[...])
        near_sum[h, 0, 0] = near[0]
        near_sum[h, 0, 1] = near[1]
        near_sum[h, 1, 0] = near[2][rows:] + own[2][:rows]
        near_sum[h, 1, 1] = near[3][rows:] + own[3][:rows]
        own_sum[h, 0, 0] = own[0]
        own_sum[h, 0, 1] = own[1]
        own_sum[h, 1, 0] = own[2][rows:]
        own_sum[h, 1, 1] = own[3][rows:]

    def relay(h):
        for c in far_returns(h):
            c.wait_recv()
        near_out[h] = (near_sum[h] + far_in[h].astype(jnp.float32)).astype(jnp.bfloat16)
        for c in near_returns(h):
            c.start()

    def finish(g):
        for i in range(group_heads):
            h = g * group_heads + i
            for c in near_returns(h):
                c.wait_recv()
            for side in range(2):
                for k in range(2):
                    total = (own_sum[h, side, k] + near_in[h, side, k].astype(jnp.float32)).astype(jnp.bfloat16)
                    mixed[pl.ds(4 * i + 2 * side + k, rows, stride=chunks), :] = dot_nn(unplace, total)
        send_group(packed_back, arrived_back, g, 1)

    def unpack_back(g):
        hand_over(arrived_back, handed_back, came_back, g, 1)

    def restore_group(g):
        hand_copy(handed_back, came_back, g, 4).wait_recv()
        for i in range(group_heads):
            lanes = pl.ds((g * group_heads + i) * HDIM, HDIM)
            for a, ref in enumerate((out_ref, grad_query_ref, grad_key_ref, grad_value_ref)):
                ref[:, lanes] = dot_nn(restore, came_back[g, 4 * i + a]).astype(jnp.bfloat16)

    unpack(0)
    place_group(0)
    each_head(0, forward)
    for g in range(1, GROUPS):
        unpack(g)
        place_group(g)
        each_head(g - 1, compute)
        if g > 1:
            finish(g - 2)
        each_head(g, forward)
        each_head(g - 1, relay)
    each_head(GROUPS - 1, compute)
    finish(GROUPS - 2)
    each_head(GROUPS - 1, relay)
    for g in range(GROUPS - 2):
        unpack_back(g)
        restore_group(g)
    finish(GROUPS - 1)
    unpack_back(GROUPS - 2)
    restore_group(GROUPS - 2)

    def settle(h):
        for c in near_copies(h) + far_copies(h) + far_returns(h) + near_returns(h):
            c.wait_send()

    for g in range(GROUPS):
        each_head(g, settle)
        wait_all(packed, 0, 0, g)
        hand_copy(handed, came, g, 3).wait_send()
    pltpu.make_async_copy(everyone, everyone, all_sems.at[0, 2, 0]).wait()
    unpack_back(GROUPS - 1)
    restore_group(GROUPS - 1)
    for g in range(GROUPS):
        wait_all(packed_back, 0, 1, g)
        hand_copy(handed_back, came_back, g, 4).wait_send()


def shards(queries, keys, values, grad_out, dest, lengths):
    _, rows, width = queries.shape
    heads = width // HDIM
    peers = lax.axis_size("dp")
    chunks = 4 * heads // GROUPS
    part = rows // peers * 2 * chunks
    blocks = lambda *lead: pltpu.VMEM((heads,) + lead + (HDIM,), jnp.bfloat16)
    totals = pltpu.VMEM((heads, 2, 2, rows, HDIM), jnp.float32)
    pieces = pltpu.VMEM((GROUPS, peers // 2, part, HDIM), jnp.bfloat16)
    handed = pltpu.VMEM((GROUPS, chunks, rows // 2, HDIM), jnp.bfloat16)
    came = pltpu.VMEM((GROUPS, chunks, rows, HDIM), jnp.bfloat16)
    slots = pltpu.VMEM((peers, 1, (rows + 127) // 128 * 256), jnp.float32)
    vmem = pl.BlockSpec(memory_space=pltpu.VMEM)
    results = pl.pallas_call(
        whole_kernel,
        out_shape=[jax.ShapeDtypeStruct((rows, width), jnp.bfloat16)] * 4,
        in_specs=[pl.BlockSpec(memory_space=pltpu.SMEM)] + [vmem] * 5,
        out_specs=[vmem] * 4,
        scratch_shapes=[
            pltpu.VMEM((peers // 2 * part, HDIM), jnp.float32),
            pieces,
            pieces,
            pieces,
            pieces,
            handed,
            came,
            handed,
            came,
            slots,
            slots,
            blocks(2, 3 * rows),
            blocks(2, 3 * rows),
            blocks(2, 2, rows),
            blocks(2, 2, rows),
            blocks(2, 2, rows),
            blocks(2, 2, rows),
            totals,
            totals,
            pltpu.VMEM((rows, 2 * rows), jnp.float32),
            pltpu.VMEM((rows, 2 * rows), jnp.float32),
            pltpu.VMEM((rows, rows), jnp.float32),
            pltpu.SemaphoreType.DMA((2, 4, heads)),
            pltpu.SemaphoreType.DMA((2, 4, heads)),
            pltpu.SemaphoreType.DMA((2, 5, GROUPS)),
        ],
        compiler_params=pltpu.CompilerParams(
            collective_id=0, has_side_effects=True, vmem_limit_bytes=52 * 1024 * 1024
        ),
        name="whole",
    )(lengths, dest, queries[0], keys[0], values[0], grad_out[0])
    return tuple(result[None] for result in results)


def solution(mesh):
    rows = P("seq", "dp", None)
    return jax.shard_map(
        shards,
        mesh=mesh,
        in_specs=(rows, rows, rows, rows, P("seq", "dp"), P("dp", None)),
        out_specs=(rows, rows, rows, rows),
        check_vma=False,
    )
```

```python
import functools

import jax
import jax.numpy as jnp
from jax import lax
from jax.experimental import pallas as pl
from jax.experimental.pallas import tpu as pltpu
from jax.sharding import PartitionSpec as P

HDIM = 128
REACH = 4
GROUPS = 4
MESH = pl.DeviceIdType.MESH


def dot_nt(a, b):
    return lax.dot_general(a, b, (((1,), (1,)), ((), ())), preferred_element_type=jnp.float32)


def dot_tn(a, b):
    return lax.dot_general(a, b, (((0,), (0,)), ((), ())), preferred_element_type=jnp.float32)


def dot_nn(a, b):
    return lax.dot_general(a, b, (((1,), (0,)), ((), ())), preferred_element_type=jnp.float32)


def pair_weight(lengths_ref, query_first, query_count, key_first, key_count):
    shape = (query_count, key_count)
    query_rows = query_first + lax.broadcasted_iota(jnp.int32, shape, 0)
    key_rows = key_first + lax.broadcasted_iota(jnp.int32, shape, 1)
    start = jnp.int32(0)
    first_rows = jnp.zeros(shape, jnp.int32)
    for c in range(lengths_ref.shape[1]):
        start = start + lengths_ref[0, c]
        first_rows = jnp.where(query_rows >= start, start, first_rows)
    mask = (key_rows >= first_rows) & (key_rows <= query_rows)
    return mask


def pair_terms(query, grad, key, value, weight):
    scale = HDIM ** (-0.5)
    scores = dot_nt(query, key) * scale
    sig = 0.5 + 0.5 * jnp.tanh(0.5 * scores)
    mixing = (scores * sig * weight).astype(jnp.bfloat16)
    grad_mix = dot_nt(grad, value)
    grad_score = (grad_mix * weight * sig * (1.0 + scores * (1.0 - sig))).astype(jnp.bfloat16)
    outputs = dot_nn(mixing, value)
    grad_query = dot_nn(grad_score, key) * scale
    grad_key = dot_tn(grad_score, query) * scale
    grad_value = dot_tn(mixing, grad)
    return outputs, grad_query, grad_key, grad_value


def whole_kernel(
    lengths_ref,
    dest_ref,
    query_ref,
    key_ref,
    value_ref,
    grad_ref,
    out_ref,
    grad_query_ref,
    grad_key_ref,
    grad_value_ref,
    loaded,
    mixed,
    packed,
    arrived,
    packed_back,
    arrived_back,
    handed,
    came,
    handed_back,
    came_back,
    slots_out,
    slots_in,
    keys,
    queries,
    far_out,
    far_in,
    near_out,
    near_in,
    near_sum,
    own_sum,
    weight_own,
    weight_near,
    weight_far,
    in_sems,
    out_sems,
    all_sems,
    load_sems,
):
    heads = keys.shape[0]
    group_heads = heads // GROUPS
    chunks = 4 * group_heads
    rows = query_ref.shape[0]
    peers = lax.axis_size("dp")
    chips = peers // 2
    per_peer = rows // peers
    part = 2 * per_peer * chunks
    shared = per_peer * chips
    me = lax.axis_index("dp")
    chip = me // 2
    core = lax.rem(me, 2)
    sibling = {"dp": 2 * chip + 1 - core}
    count = lax.axis_size("seq")
    block = lax.axis_index("seq")
    right = {"seq": lax.rem(block + 1, count)}
    left = {"seq": lax.rem(block + count - 1, count)}

    loads = [
        pltpu.make_async_copy(ref, loaded.at[a], load_sems.at[a])
        for a, ref in enumerate((query_ref, key_ref, value_ref, grad_ref))
    ]
    for c in loads:
        c.start()

    barrier = pltpu.get_barrier_semaphore()
    for neighbour in (left, right):
        pl.semaphore_signal(barrier, inc=1, device_id=neighbour, device_id_type=MESH)

    def greet(i, carry):
        pl.semaphore_signal(barrier, inc=1, device_id={"dp": lax.rem(me + i, peers)}, device_id_type=MESH)
        return carry

    lax.fori_loop(1, peers, greet, 0)

    def copy(src, dst, sems, which, h, target):
        return pltpu.make_async_remote_copy(
            src_ref=src,
            dst_ref=dst,
            send_sem=sems.at[0, which, h],
            recv_sem=sems.at[1, which, h],
            device_id=target,
            device_id_type=MESH,
        )

    def near_copies(h):
        return (
            copy(keys.at[h, :, pl.ds(2 * rows, rows)], keys.at[h, :, pl.ds(rows, rows)], in_sems, 0, h, right),
            copy(queries.at[h, :, pl.ds(0, rows)], queries.at[h, :, pl.ds(rows, rows)], in_sems, 1, h, left),
        )

    def far_copies(h):
        return (
            copy(keys.at[h, :, pl.ds(rows, rows)], keys.at[h, :, pl.ds(0, rows)], in_sems, 2, h, right),
            copy(queries.at[h, :, pl.ds(rows, rows)], queries.at[h, :, pl.ds(2 * rows, rows)], in_sems, 3, h, left),
        )

    def far_returns(h):
        return (
            copy(far_out.at[h, 0], far_in.at[h, 0], out_sems, 0, h, right),
            copy(far_out.at[h, 1], far_in.at[h, 1], out_sems, 1, h, left),
        )

    def near_returns(h):
        return (
            copy(near_out.at[h, 0], near_in.at[h, 0], out_sems, 2, h, right),
            copy(near_out.at[h, 1], near_in.at[h, 1], out_sems, 3, h, left),
        )

    def send_group(source, target, g, which):
        def send(i, carry):
            other = lax.rem(chip + i, chips)
            source[g, other] = mixed[pl.ds(pl.multiple_of(other * part, 16), part), :].astype(jnp.bfloat16)
            copy(source.at[g, other], target.at[g, chip], all_sems, which, g, {"dp": 2 * other + core}).start()
            return carry

        lax.fori_loop(1, chips, send, 0)
        target[g, chip] = mixed[pl.ds(pl.multiple_of(chip * part, 16), part), :].astype(jnp.bfloat16)

    def wait_all(ref, side, which, g):
        whole = ref.at[g, pl.ds(0, chips - 1)]
        pltpu.make_async_copy(whole, whole, all_sems.at[side, which, g]).wait()

    def hand_copy(source, target, g, which):
        return copy(source.at[g], target.at[g, :, pl.ds(shared, shared)], all_sems, which, g, sibling)

    def hand_over(source, given, target, g, which):
        wait_all(source, 1, which, g)
        mixed[...] = source[g].reshape(chips * part, HDIM).astype(jnp.float32)
        for c in range(chunks):
            for t in range(per_peer):
                first = mixed[pl.ds(t * chunks + c, chips, stride=part), :]
                second = mixed[pl.ds((per_peer + t) * chunks + c, chips, stride=part), :]
                given[g, c, pl.ds(t * chips, chips), :] = jnp.where(core == 0, second, first).astype(jnp.bfloat16)
        hand_copy(given, target, g, which + 3).start()
        for c in range(chunks):
            for t in range(per_peer):
                first = mixed[pl.ds(t * chunks + c, chips, stride=part), :]
                second = mixed[pl.ds((per_peer + t) * chunks + c, chips, stride=part), :]
                target[g, c, pl.ds(t * chips, chips), :] = jnp.where(core == 0, first, second).astype(jnp.bfloat16)

    targets = dest_ref[...].astype(jnp.float32)
    across = jnp.broadcast_to(targets, (rows, rows))
    ranks = jnp.sum(jnp.where(across.T < across, jnp.float32(1.0), jnp.float32(0.0)), axis=0, keepdims=True)
    steps = lax.broadcasted_iota(jnp.int32, (rows, rows), 0).astype(jnp.float32)
    order = jnp.where(steps == ranks, jnp.float32(1.0), jnp.float32(0.0)).astype(jnp.bfloat16)
    holder = jnp.floor((ranks + 0.5) * (1.0 / per_peer))
    holder_chip = jnp.floor((holder + 0.5) * 0.5)
    away = jnp.abs(holder - 2.0 * holder_chip - core.astype(jnp.float32))
    spots = away * shared + (ranks - holder * per_peer) * chips + holder_chip
    restore = jnp.where(steps == spots, jnp.float32(1.0), jnp.float32(0.0)).T.astype(jnp.bfloat16)

    def pack_group(g):
        for a in range(4):
            sorted_rows = dot_nn(order, loaded[a, :, pl.ds(g * group_heads * HDIM, group_heads * HDIM)])
            for i in range(group_heads):
                mixed[pl.ds(4 * i + a, rows, stride=chunks), :] = sorted_rows[:, i * HDIM : (i + 1) * HDIM]
        if g == 0:
            pl.semaphore_wait(barrier, peers + 1)
        send_group(packed, arrived, g, 0)

    width = slots_out.shape[2]
    lane = lax.broadcasted_iota(jnp.int32, (peers, 1, width), 2)
    receiver = lax.broadcasted_iota(jnp.int32, (peers, 1, 1), 0)
    apart = jnp.where(lax.rem(receiver, 2) == core, 0, shared)
    slots = jnp.zeros((peers, 1, width), jnp.float32)
    base = (receiver * rows).astype(jnp.float32)
    first_rank = (receiver * per_peer).astype(jnp.float32)
    for t in range(per_peer):
        hit = ranks.reshape(1, 1, rows) == first_rank + t
        slot = jnp.sum(jnp.where(hit, targets.reshape(1, 1, rows), jnp.float32(0.0)), axis=2, keepdims=True) - base
        slots = jnp.where(lane == apart + t * chips + chip, slot, slots)
        slots = jnp.where(lane == width // 2 + me * per_peer + t, slot, slots)
    slots_out[...] = slots

    for c in loads:
        c.wait()
    pack_group(0)
    def send_slots(i, carry):
        peer = lax.rem(me + i, peers)
        copy(slots_out.at[peer], slots_in.at[me], all_sems, 2, 0, {"dp": peer}).start()
        return carry

    lax.fori_loop(1, peers, send_slots, 0)
    slots_in[me] = slots_out[me]

    for g in range(1, GROUPS):
        pack_group(g)

    weight = jnp.float32(1.0 / (REACH * rows))
    first = block * rows
    for ref, query_first, key_first in (
        (weight_own, first, first - rows),
        (weight_near, first + rows, first - 2 * rows),
        (weight_far, first + 2 * rows, first - 2 * rows),
    ):
        mask = pair_weight(lengths_ref, query_first, ref.shape[0], key_first, ref.shape[1])
        ref[...] = jnp.where(mask, weight, jnp.float32(0.0))

    everyone = slots_in.at[pl.ds(0, peers - 1)]
    pltpu.make_async_copy(everyone, everyone, all_sems.at[1, 2, 0]).wait()
    slot_row = jnp.sum(slots_in[...], axis=0)
    place = jnp.where(steps == slot_row[:, :rows], jnp.float32(1.0), jnp.float32(0.0)).astype(jnp.bfloat16)
    back = slot_row[:, width // 2 : width // 2 + rows]
    unplace = jnp.where(steps == back, jnp.float32(1.0), jnp.float32(0.0)).T.astype(jnp.bfloat16)

    def each_head(g, step):
        def run(h, carry):
            step(h)
            return carry

        lax.fori_loop(g * group_heads, (g + 1) * group_heads, run, 0)

    def unpack(g):
        hand_over(arrived, handed, came, g, 0)

    def place_group(g):
        hand_copy(handed, came, g, 3).wait_recv()
        for i in range(group_heads):
            h = g * group_heads + i
            for a, (buffer, k, start) in enumerate(
                ((queries, 0, 0), (keys, 0, 2 * rows), (keys, 1, 2 * rows), (queries, 1, 0))
            ):
                buffer[h, k, pl.ds(start, rows), :] = dot_nn(place, came[g, 4 * i + a]).astype(jnp.bfloat16)
            for c in near_copies(h):
                c.start()

    def forward(h):
        for c in near_copies(h):
            c.wait_recv()
        for c in far_copies(h):
            c.start()

    def compute(h):
        for c in far_copies(h):
            c.wait_recv()
        key, value = keys[h, 0], keys[h, 1]
        query, grad = queries[h, 0], queries[h, 1]
        far = pair_terms(query[2 * rows :], grad[2 * rows :], key[:rows], value[:rows], weight_far[...])
        near = pair_terms(
            query[rows : 2 * rows], grad[rows : 2 * rows], key[: 2 * rows], value[: 2 * rows], weight_near[...]
        )
        far_out[h, 0, 0] = far[0].astype(jnp.bfloat16)
        far_out[h, 0, 1] = far[1].astype(jnp.bfloat16)
        far_out[h, 1, 0] = (far[2] + near[2][:rows]).astype(jnp.bfloat16)
        far_out[h, 1, 1] = (far[3] + near[3][:rows]).astype(jnp.bfloat16)
        for c in far_returns(h):
            c.start()
        own = pair_terms(query[:rows], grad[:rows], key[rows:], value[rows:], weight_own[...])
        near_sum[h, 0, 0] = near[0]
        near_sum[h, 0, 1] = near[1]
        near_sum[h, 1, 0] = near[2][rows:] + own[2][:rows]
        near_sum[h, 1, 1] = near[3][rows:] + own[3][:rows]
        own_sum[h, 0, 0] = own[0]
        own_sum[h, 0, 1] = own[1]
        own_sum[h, 1, 0] = own[2][rows:]
        own_sum[h, 1, 1] = own[3][rows:]

    def relay(h):
        for c in far_returns(h):
            c.wait_recv()
        near_out[h] = (near_sum[h] + far_in[h].astype(jnp.float32)).astype(jnp.bfloat16)
        for c in near_returns(h):
            c.start()

    def finish(g):
        for i in range(group_heads):
            h = g * group_heads + i
            for c in near_returns(h):
                c.wait_recv()
            for side in range(2):
                for k in range(2):
                    total = (own_sum[h, side, k] + near_in[h, side, k].astype(jnp.float32)).astype(jnp.bfloat16)
                    mixed[pl.ds(4 * i + 2 * side + k, rows, stride=chunks), :] = dot_nn(unplace, total)
        send_group(packed_back, arrived_back, g, 1)

    def unpack_back(g):
        hand_over(arrived_back, handed_back, came_back, g, 1)

    def restore_group(g):
        hand_copy(handed_back, came_back, g, 4).wait_recv()
        for i in range(group_heads):
            lanes = pl.ds((g * group_heads + i) * HDIM, HDIM)
            for a, ref in enumerate((out_ref, grad_query_ref, grad_key_ref, grad_value_ref)):
                ref[:, lanes] = dot_nn(restore, came_back[g, 4 * i + a]).astype(jnp.bfloat16)

    unpack(0)
    place_group(0)
    each_head(0, forward)
    for g in range(1, GROUPS):
        unpack(g)
        place_group(g)
        each_head(g - 1, compute)
        if g > 1:
            finish(g - 2)
        each_head(g, forward)
        each_head(g - 1, relay)
    each_head(GROUPS - 1, compute)
    finish(GROUPS - 2)
    each_head(GROUPS - 1, relay)
    for g in range(GROUPS - 2):
        unpack_back(g)
        restore_group(g)
    finish(GROUPS - 1)
    unpack_back(GROUPS - 2)
    restore_group(GROUPS - 2)

    def settle(h):
        for c in near_copies(h) + far_copies(h) + far_returns(h) + near_returns(h):
            c.wait_send()

    for g in range(GROUPS):
        each_head(g, settle)
        wait_all(packed, 0, 0, g)
        hand_copy(handed, came, g, 3).wait_send()
    pltpu.make_async_copy(everyone, everyone, all_sems.at[0, 2, 0]).wait()
    unpack_back(GROUPS - 1)
    restore_group(GROUPS - 1)
    for g in range(GROUPS):
        wait_all(packed_back, 0, 1, g)
        hand_copy(handed_back, came_back, g, 4).wait_send()


def deliver_kernel(*refs):
    sems = refs[-1]
    moves = [pltpu.make_async_copy(refs[a], refs[4 + a], sems.at[a]) for a in range(4)]
    for move in moves:
        move.start()
    for move in moves:
        move.wait()


def shards(queries, keys, values, grad_out, dest, lengths):
    _, rows, width = queries.shape
    heads = width // HDIM
    peers = lax.axis_size("dp")
    chunks = 4 * heads // GROUPS
    part = rows // peers * 2 * chunks
    blocks = lambda *lead: pltpu.VMEM((heads,) + lead + (HDIM,), jnp.bfloat16)
    totals = pltpu.VMEM((heads, 2, 2, rows, HDIM), jnp.float32)
    pieces = pltpu.VMEM((GROUPS, peers // 2, part, HDIM), jnp.bfloat16)
    handed = pltpu.VMEM((GROUPS, chunks, rows // 2, HDIM), jnp.bfloat16)
    came = pltpu.VMEM((GROUPS, chunks, rows, HDIM), jnp.bfloat16)
    slots = pltpu.VMEM((peers, 1, (rows + 127) // 128 * 256), jnp.float32)
    vmem = pl.BlockSpec(memory_space=pltpu.VMEM)
    results = pl.pallas_call(
        whole_kernel,
        out_shape=[jax.ShapeDtypeStruct((rows, width), jnp.bfloat16)] * 4,
        in_specs=[pl.BlockSpec(memory_space=pltpu.SMEM), vmem] + [pl.BlockSpec(memory_space=pltpu.HBM)] * 4,
        out_specs=[vmem] * 4,
        scratch_shapes=[
            pltpu.VMEM((4, rows, width), jnp.bfloat16),
            pltpu.VMEM((peers // 2 * part, HDIM), jnp.float32),
            pieces,
            pieces,
            pieces,
            pieces,
            handed,
            came,
            handed,
            came,
            slots,
            slots,
            blocks(2, 3 * rows),
            blocks(2, 3 * rows),
            blocks(2, 2, rows),
            blocks(2, 2, rows),
            blocks(2, 2, rows),
            blocks(2, 2, rows),
            totals,
            totals,
            pltpu.VMEM((rows, 2 * rows), jnp.float32),
            pltpu.VMEM((rows, 2 * rows), jnp.float32),
            pltpu.VMEM((rows, rows), jnp.float32),
            pltpu.SemaphoreType.DMA((2, 4, heads)),
            pltpu.SemaphoreType.DMA((2, 4, heads)),
            pltpu.SemaphoreType.DMA((2, 5, GROUPS)),
            pltpu.SemaphoreType.DMA((4,)),
        ],
        compiler_params=pltpu.CompilerParams(
            collective_id=0, has_side_effects=True, vmem_limit_bytes=52 * 1024 * 1024
        ),
        name="whole",
    )(lengths, dest, queries[0], keys[0], values[0], grad_out[0])
    anywhere = [pl.BlockSpec(memory_space=pl.ANY)] * 4
    results = pl.pallas_call(
        deliver_kernel,
        out_shape=[jax.ShapeDtypeStruct((rows, width), jnp.bfloat16)] * 4,
        in_specs=anywhere,
        out_specs=anywhere,
        scratch_shapes=[pltpu.SemaphoreType.DMA((4,))],
        name="deliver",
    )(*results)
    return tuple(result[None] for result in results)


def solution(mesh):
    rows = P("seq", "dp", None)
    return jax.shard_map(
        shards,
        mesh=mesh,
        in_specs=(rows, rows, rows, rows, P("seq", "dp"), P("dp", None)),
        out_specs=(rows, rows, rows, rows),
        check_vma=False,
    )
```

```python
import functools

import jax
import jax.numpy as jnp
from jax import lax
from jax.experimental import pallas as pl
from jax.experimental.pallas import tpu as pltpu
from jax.sharding import PartitionSpec as P

HDIM = 128
REACH = 4
SIZES = (1, 2, 2, 2, 1)
GROUPS = len(SIZES)
MESH = pl.DeviceIdType.MESH


def dot_nt(a, b):
    return lax.dot_general(a, b, (((1,), (1,)), ((), ())), preferred_element_type=jnp.float32)


def dot_tn(a, b):
    return lax.dot_general(a, b, (((0,), (0,)), ((), ())), preferred_element_type=jnp.float32)


def dot_nn(a, b):
    return lax.dot_general(a, b, (((1,), (0,)), ((), ())), preferred_element_type=jnp.float32)


def pair_weight(lengths_ref, query_first, query_count, key_first, key_count):
    shape = (query_count, key_count)
    query_rows = query_first + lax.broadcasted_iota(jnp.int32, shape, 0)
    key_rows = key_first + lax.broadcasted_iota(jnp.int32, shape, 1)
    start = jnp.int32(0)
    first_rows = jnp.zeros(shape, jnp.int32)
    for c in range(lengths_ref.shape[1]):
        start = start + lengths_ref[0, c]
        first_rows = jnp.where(query_rows >= start, start, first_rows)
    mask = (key_rows >= first_rows) & (key_rows <= query_rows)
    return mask


def pair_terms(query, grad, key, value, weight):
    scale = HDIM ** (-0.5)
    scores = dot_nt(query, key) * scale
    sig = 0.5 + 0.5 * jnp.tanh(0.5 * scores)
    mixing = (scores * sig * weight).astype(jnp.bfloat16)
    grad_mix = dot_nt(grad, value)
    grad_score = (grad_mix * weight * sig * (1.0 + scores * (1.0 - sig))).astype(jnp.bfloat16)
    outputs = dot_nn(mixing, value)
    grad_query = dot_nn(grad_score, key) * scale
    grad_key = dot_tn(grad_score, query) * scale
    grad_value = dot_tn(mixing, grad)
    return outputs, grad_query, grad_key, grad_value


def whole_kernel(
    lengths_ref,
    dest_ref,
    query_ref,
    key_ref,
    value_ref,
    grad_ref,
    out_ref,
    grad_query_ref,
    grad_key_ref,
    grad_value_ref,
    loaded,
    mixed,
    packed,
    arrived,
    packed_back,
    arrived_back,
    handed,
    came,
    handed_back,
    came_back,
    slots_out,
    slots_in,
    keys,
    queries,
    far_out,
    far_in,
    near_out,
    near_in,
    near_sum,
    own_sum,
    weight_own,
    weight_near,
    weight_far,
    in_sems,
    out_sems,
    all_sems,
    load_sems,
):
    heads = keys.shape[0]
    rows = query_ref.shape[0]
    peers = lax.axis_size("dp")
    chips = peers // 2
    per_peer = rows // peers
    shared = per_peer * chips
    firsts = [sum(SIZES[:g]) for g in range(GROUPS)]
    parts = [(2 * per_peer * 4 * size + 15) // 16 * 16 for size in SIZES]
    me = lax.axis_index("dp")
    chip = me // 2
    core = lax.rem(me, 2)
    sibling = {"dp": 2 * chip + 1 - core}
    count = lax.axis_size("seq")
    block = lax.axis_index("seq")
    right = {"seq": lax.rem(block + 1, count)}
    left = {"seq": lax.rem(block + count - 1, count)}

    loads = [
        pltpu.make_async_copy(ref, loaded.at[a], load_sems.at[a])
        for a, ref in enumerate((query_ref, key_ref, value_ref, grad_ref))
    ]
    for c in loads:
        c.start()

    barrier = pltpu.get_barrier_semaphore()
    for neighbour in (left, right):
        pl.semaphore_signal(barrier, inc=1, device_id=neighbour, device_id_type=MESH)

    def greet(i, carry):
        pl.semaphore_signal(barrier, inc=1, device_id={"dp": lax.rem(me + i, peers)}, device_id_type=MESH)
        return carry

    lax.fori_loop(1, peers, greet, 0)

    def copy(src, dst, sems, which, h, target):
        return pltpu.make_async_remote_copy(
            src_ref=src,
            dst_ref=dst,
            send_sem=sems.at[0, which, h],
            recv_sem=sems.at[1, which, h],
            device_id=target,
            device_id_type=MESH,
        )

    def near_copies(h):
        return (
            copy(keys.at[h, :, pl.ds(2 * rows, rows)], keys.at[h, :, pl.ds(rows, rows)], in_sems, 0, h, right),
            copy(queries.at[h, :, pl.ds(0, rows)], queries.at[h, :, pl.ds(rows, rows)], in_sems, 1, h, left),
        )

    def far_copies(h):
        return (
            copy(keys.at[h, :, pl.ds(rows, rows)], keys.at[h, :, pl.ds(0, rows)], in_sems, 2, h, right),
            copy(queries.at[h, :, pl.ds(rows, rows)], queries.at[h, :, pl.ds(2 * rows, rows)], in_sems, 3, h, left),
        )

    def far_returns(h):
        return (
            copy(far_out.at[h, 0], far_in.at[h, 0], out_sems, 0, h, right),
            copy(far_out.at[h, 1], far_in.at[h, 1], out_sems, 1, h, left),
        )

    def near_returns(h):
        return (
            copy(near_out.at[h, 0], near_in.at[h, 0], out_sems, 2, h, right),
            copy(near_out.at[h, 1], near_in.at[h, 1], out_sems, 3, h, left),
        )

    def send_group(source, target, g, which):
        part = parts[g]

        def send(i, carry):
            other = lax.rem(chip + i, chips)
            source[g, other, pl.ds(0, part), :] = mixed[pl.ds(pl.multiple_of(other * part, 16), part), :].astype(jnp.bfloat16)
            piece, place_there = source.at[g, other, pl.ds(0, part)], target.at[g, chip, pl.ds(0, part)]
            copy(piece, place_there, all_sems, which, g, {"dp": 2 * other + core}).start()
            return carry

        lax.fori_loop(1, chips, send, 0)
        target[g, chip, pl.ds(0, part), :] = mixed[pl.ds(pl.multiple_of(chip * part, 16), part), :].astype(jnp.bfloat16)

    def wait_all(ref, side, which, g):
        whole = ref.at[g, pl.ds(0, chips - 1), pl.ds(0, parts[g])]
        pltpu.make_async_copy(whole, whole, all_sems.at[side, which, g]).wait()

    def hand_copy(source, target, g, which):
        used = pl.ds(0, 4 * SIZES[g])
        return copy(source.at[g, used], target.at[g, used, pl.ds(shared, shared)], all_sems, which, g, sibling)

    def hand_over(source, given, target, g, which):
        wait_all(source, 1, which, g)
        part, chunks = parts[g], 4 * SIZES[g]
        came_rows = source[g, :, pl.ds(0, part), :].reshape(chips * part, HDIM)
        mixed[pl.ds(0, chips * part), :] = came_rows.astype(jnp.float32)
        for c in range(chunks):
            for t in range(per_peer):
                first = mixed[pl.ds(t * chunks + c, chips, stride=part), :]
                second = mixed[pl.ds((per_peer + t) * chunks + c, chips, stride=part), :]
                given[g, c, pl.ds(t * chips, chips), :] = jnp.where(core == 0, second, first).astype(jnp.bfloat16)
        hand_copy(given, target, g, which + 3).start()
        for c in range(chunks):
            for t in range(per_peer):
                first = mixed[pl.ds(t * chunks + c, chips, stride=part), :]
                second = mixed[pl.ds((per_peer + t) * chunks + c, chips, stride=part), :]
                target[g, c, pl.ds(t * chips, chips), :] = jnp.where(core == 0, first, second).astype(jnp.bfloat16)

    targets = dest_ref[...].astype(jnp.float32)
    across = jnp.broadcast_to(targets, (rows, rows))
    ranks = jnp.sum(jnp.where(across.T < across, jnp.float32(1.0), jnp.float32(0.0)), axis=0, keepdims=True)
    steps = lax.broadcasted_iota(jnp.int32, (rows, rows), 0).astype(jnp.float32)
    holder = jnp.floor((ranks + 0.5) * (1.0 / per_peer))
    holder_chip = jnp.floor((holder + 0.5) * 0.5)
    mailed = (ranks - holder_chip * (2 * per_peer)) * chips + holder_chip
    order = jnp.where(steps == mailed, jnp.float32(1.0), jnp.float32(0.0)).astype(jnp.bfloat16)
    away = jnp.abs(holder - 2.0 * holder_chip - core.astype(jnp.float32))
    spots = away * shared + (ranks - holder * per_peer) * chips + holder_chip
    restore = jnp.where(steps == spots, jnp.float32(1.0), jnp.float32(0.0)).T.astype(jnp.bfloat16)

    mixed[...] = jnp.zeros_like(mixed)

    def mix(g, c, values):
        for u in range(2 * per_peer):
            mixed[pl.ds(u * 4 * SIZES[g] + c, chips, stride=parts[g]), :] = values[u * chips : (u + 1) * chips]

    def pack_group(g):
        for a in range(4):
            sorted_rows = dot_nn(order, loaded[a, :, pl.ds(firsts[g] * HDIM, SIZES[g] * HDIM)])
            for i in range(SIZES[g]):
                mix(g, 4 * i + a, sorted_rows[:, i * HDIM : (i + 1) * HDIM])
        if g == 0:
            pl.semaphore_wait(barrier, peers + 1)
        send_group(packed, arrived, g, 0)

    width = slots_out.shape[2]
    lane = lax.broadcasted_iota(jnp.int32, (peers, 1, width), 2)
    receiver = lax.broadcasted_iota(jnp.int32, (peers, 1, 1), 0)
    apart = jnp.where(lax.rem(receiver, 2) == core, 0, shared)
    slots = jnp.zeros((peers, 1, width), jnp.float32)
    base = (receiver * rows).astype(jnp.float32)
    first_rank = (receiver * per_peer).astype(jnp.float32)
    for t in range(per_peer):
        hit = ranks.reshape(1, 1, rows) == first_rank + t
        slot = jnp.sum(jnp.where(hit, targets.reshape(1, 1, rows), jnp.float32(0.0)), axis=2, keepdims=True) - base
        slots = jnp.where(lane == apart + t * chips + chip, slot, slots)
        slots = jnp.where(lane == width // 2 + (core * per_peer + t) * chips + chip, slot, slots)
    slots_out[...] = slots

    for c in loads:
        c.wait()
    pack_group(0)
    def send_slots(i, carry):
        peer = lax.rem(me + i, peers)
        copy(slots_out.at[peer], slots_in.at[me], all_sems, 2, 0, {"dp": peer}).start()
        return carry

    lax.fori_loop(1, peers, send_slots, 0)
    slots_in[me] = slots_out[me]

    for g in range(1, GROUPS):
        pack_group(g)

    weight = jnp.float32(1.0 / (REACH * rows))
    first = block * rows
    for ref, query_first, key_first in (
        (weight_own, first, first - rows),
        (weight_near, first + rows, first - 2 * rows),
        (weight_far, first + 2 * rows, first - 2 * rows),
    ):
        mask = pair_weight(lengths_ref, query_first, ref.shape[0], key_first, ref.shape[1])
        ref[...] = jnp.where(mask, weight, jnp.float32(0.0))

    everyone = slots_in.at[pl.ds(0, peers - 1)]
    pltpu.make_async_copy(everyone, everyone, all_sems.at[1, 2, 0]).wait()
    slot_row = jnp.sum(slots_in[...], axis=0)
    place = jnp.where(steps == slot_row[:, :rows], jnp.float32(1.0), jnp.float32(0.0)).astype(jnp.bfloat16)
    back = slot_row[:, width // 2 : width // 2 + rows]
    unplace = jnp.where(steps == back, jnp.float32(1.0), jnp.float32(0.0)).T.astype(jnp.bfloat16)

    def each_head(g, step):
        def run(h, carry):
            step(h)
            return carry

        lax.fori_loop(firsts[g], firsts[g] + SIZES[g], run, 0)

    def unpack(g):
        hand_over(arrived, handed, came, g, 0)

    def place_group(g):
        hand_copy(handed, came, g, 3).wait_recv()
        for i in range(SIZES[g]):
            h = firsts[g] + i
            for a, (buffer, k, start) in enumerate(
                ((queries, 0, 0), (keys, 0, 2 * rows), (keys, 1, 2 * rows), (queries, 1, 0))
            ):
                buffer[h, k, pl.ds(start, rows), :] = dot_nn(place, came[g, 4 * i + a]).astype(jnp.bfloat16)
            for c in near_copies(h):
                c.start()

    def forward(h):
        for c in near_copies(h):
            c.wait_recv()
        for c in far_copies(h):
            c.start()

    def compute(h):
        for c in far_copies(h):
            c.wait_recv()
        key, value = keys[h, 0], keys[h, 1]
        query, grad = queries[h, 0], queries[h, 1]
        far = pair_terms(query[2 * rows :], grad[2 * rows :], key[:rows], value[:rows], weight_far[...])
        near = pair_terms(
            query[rows : 2 * rows], grad[rows : 2 * rows], key[: 2 * rows], value[: 2 * rows], weight_near[...]
        )
        far_out[h, 0, 0] = far[0].astype(jnp.bfloat16)
        far_out[h, 0, 1] = far[1].astype(jnp.bfloat16)
        far_out[h, 1, 0] = (far[2] + near[2][:rows]).astype(jnp.bfloat16)
        far_out[h, 1, 1] = (far[3] + near[3][:rows]).astype(jnp.bfloat16)
        for c in far_returns(h):
            c.start()
        own = pair_terms(query[:rows], grad[:rows], key[rows:], value[rows:], weight_own[...])
        near_sum[h, 0, 0] = near[0]
        near_sum[h, 0, 1] = near[1]
        near_sum[h, 1, 0] = near[2][rows:] + own[2][:rows]
        near_sum[h, 1, 1] = near[3][rows:] + own[3][:rows]
        own_sum[h, 0, 0] = own[0]
        own_sum[h, 0, 1] = own[1]
        own_sum[h, 1, 0] = own[2][rows:]
        own_sum[h, 1, 1] = own[3][rows:]

    def relay(h):
        for c in far_returns(h):
            c.wait_recv()
        near_out[h] = (near_sum[h] + far_in[h].astype(jnp.float32)).astype(jnp.bfloat16)
        for c in near_returns(h):
            c.start()

    def finish(g):
        for i in range(SIZES[g]):
            h = firsts[g] + i
            for c in near_returns(h):
                c.wait_recv()
            for side in range(2):
                for k in range(2):
                    total = (own_sum[h, side, k] + near_in[h, side, k].astype(jnp.float32)).astype(jnp.bfloat16)
                    mix(g, 4 * i + 2 * side + k, dot_nn(unplace, total))
        send_group(packed_back, arrived_back, g, 1)

    def unpack_back(g):
        hand_over(arrived_back, handed_back, came_back, g, 1)

    def restore_group(g):
        hand_copy(handed_back, came_back, g, 4).wait_recv()
        for i in range(SIZES[g]):
            lanes = pl.ds((firsts[g] + i) * HDIM, HDIM)
            for a, ref in enumerate((out_ref, grad_query_ref, grad_key_ref, grad_value_ref)):
                ref[:, lanes] = dot_nn(restore, came_back[g, 4 * i + a]).astype(jnp.bfloat16)

    unpack(0)
    place_group(0)
    each_head(0, forward)
    for g in range(1, GROUPS):
        unpack(g)
        place_group(g)
        each_head(g - 1, compute)
        if g > 1:
            finish(g - 2)
        each_head(g, forward)
        each_head(g - 1, relay)
        if g > 2:
            unpack_back(g - 3)
            restore_group(g - 3)
    each_head(GROUPS - 1, compute)
    finish(GROUPS - 2)
    each_head(GROUPS - 1, relay)
    finish(GROUPS - 1)
    for g in range(GROUPS - 3, GROUPS - 1):
        unpack_back(g)
        restore_group(g)

    def settle(h):
        for c in near_copies(h) + far_copies(h) + far_returns(h) + near_returns(h):
            c.wait_send()

    for g in range(GROUPS):
        each_head(g, settle)
        wait_all(packed, 0, 0, g)
        hand_copy(handed, came, g, 3).wait_send()
    pltpu.make_async_copy(everyone, everyone, all_sems.at[0, 2, 0]).wait()
    unpack_back(GROUPS - 1)
    restore_group(GROUPS - 1)
    for g in range(GROUPS):
        wait_all(packed_back, 0, 1, g)
        hand_copy(handed_back, came_back, g, 4).wait_send()


def shards(queries, keys, values, grad_out, dest, lengths):
    _, rows, width = queries.shape
    heads = width // HDIM
    peers = lax.axis_size("dp")
    chunks = 4 * max(SIZES)
    part = rows // peers * 2 * chunks
    blocks = lambda *lead: pltpu.VMEM((heads,) + lead + (HDIM,), jnp.bfloat16)
    totals = pltpu.VMEM((heads, 2, 2, rows, HDIM), jnp.float32)
    pieces = pltpu.VMEM((GROUPS, peers // 2, part, HDIM), jnp.bfloat16)
    handed = pltpu.VMEM((GROUPS, chunks, rows // 2, HDIM), jnp.bfloat16)
    came = pltpu.VMEM((GROUPS, chunks, rows, HDIM), jnp.bfloat16)
    slots = pltpu.VMEM((peers, 1, (rows + 127) // 128 * 256), jnp.float32)
    vmem = pl.BlockSpec(memory_space=pltpu.VMEM)
    results = pl.pallas_call(
        whole_kernel,
        out_shape=[jax.ShapeDtypeStruct((rows, width), jnp.bfloat16)] * 4,
        in_specs=[pl.BlockSpec(memory_space=pltpu.SMEM), vmem] + [pl.BlockSpec(memory_space=pltpu.HBM)] * 4,
        out_specs=[vmem] * 4,
        scratch_shapes=[
            pltpu.VMEM((4, rows, width), jnp.bfloat16),
            pltpu.VMEM((peers // 2 * part, HDIM), jnp.float32),
            pieces,
            pieces,
            pieces,
            pieces,
            handed,
            came,
            handed,
            came,
            slots,
            slots,
            blocks(2, 3 * rows),
            blocks(2, 3 * rows),
            blocks(2, 2, rows),
            blocks(2, 2, rows),
            blocks(2, 2, rows),
            blocks(2, 2, rows),
            totals,
            totals,
            pltpu.VMEM((rows, 2 * rows), jnp.float32),
            pltpu.VMEM((rows, 2 * rows), jnp.float32),
            pltpu.VMEM((rows, rows), jnp.float32),
            pltpu.SemaphoreType.DMA((2, 4, heads)),
            pltpu.SemaphoreType.DMA((2, 4, heads)),
            pltpu.SemaphoreType.DMA((2, 5, GROUPS)),
            pltpu.SemaphoreType.DMA((4,)),
        ],
        compiler_params=pltpu.CompilerParams(
            collective_id=0, has_side_effects=True, vmem_limit_bytes=52 * 1024 * 1024
        ),
        name="whole",
    )(lengths, dest, queries[0], keys[0], values[0], grad_out[0])
    return tuple(result[None] for result in results)


def solution(mesh):
    rows = P("seq", "dp", None)
    return jax.shard_map(
        shards,
        mesh=mesh,
        in_specs=(rows, rows, rows, rows, P("seq", "dp"), P("dp", None)),
        out_specs=(rows, rows, rows, rows),
        check_vma=False,
    )
```

```python
import functools

import jax
import jax.numpy as jnp
from jax import lax
from jax.experimental import pallas as pl
from jax.experimental.pallas import tpu as pltpu
from jax.sharding import PartitionSpec as P

HDIM = 128
REACH = 4
SIZES = (1, 2, 2, 2, 1)
GROUPS = len(SIZES)
MESH = pl.DeviceIdType.MESH


def dot_nt(a, b):
    return lax.dot_general(a, b, (((1,), (1,)), ((), ())), preferred_element_type=jnp.float32)


def dot_tn(a, b):
    return lax.dot_general(a, b, (((0,), (0,)), ((), ())), preferred_element_type=jnp.float32)


def dot_nn(a, b):
    return lax.dot_general(a, b, (((1,), (0,)), ((), ())), preferred_element_type=jnp.float32)


def pair_weight(lengths_ref, query_first, query_count, key_first, key_count):
    shape = (query_count, key_count)
    query_rows = query_first + lax.broadcasted_iota(jnp.int32, shape, 0)
    key_rows = key_first + lax.broadcasted_iota(jnp.int32, shape, 1)
    start = jnp.int32(0)
    first_rows = jnp.zeros(shape, jnp.int32)
    for c in range(lengths_ref.shape[1]):
        start = start + lengths_ref[0, c]
        first_rows = jnp.where(query_rows >= start, start, first_rows)
    mask = (key_rows >= first_rows) & (key_rows <= query_rows)
    return mask


def pair_terms(query, grad, key, value, weight):
    scale = HDIM ** (-0.5)
    scores = dot_nt(query, key) * scale
    sig = 0.5 + 0.5 * jnp.tanh(0.5 * scores)
    mixing = (scores * sig * weight).astype(jnp.bfloat16)
    grad_mix = dot_nt(grad, value)
    grad_score = (grad_mix * weight * sig * (1.0 + scores * (1.0 - sig))).astype(jnp.bfloat16)
    outputs = dot_nn(mixing, value)
    grad_query = dot_nn(grad_score, key) * scale
    grad_key = dot_tn(grad_score, query) * scale
    grad_value = dot_tn(mixing, grad)
    return outputs, grad_query, grad_key, grad_value


def whole_kernel(
    lengths_ref,
    dest_ref,
    query_ref,
    key_ref,
    value_ref,
    grad_ref,
    out_ref,
    grad_query_ref,
    grad_key_ref,
    grad_value_ref,
    loaded,
    mixed,
    packed,
    arrived,
    packed_back,
    arrived_back,
    handed,
    came,
    handed_back,
    came_back,
    slots_out,
    slots_in,
    keys,
    queries,
    far_out,
    far_in,
    near_out,
    near_in,
    near_sum,
    own_sum,
    weight_own,
    weight_near,
    weight_far,
    in_sems,
    out_sems,
    all_sems,
    load_sems,
):
    heads = keys.shape[0]
    rows = query_ref.shape[0]
    peers = lax.axis_size("dp")
    chips = peers // 2
    per_peer = rows // peers
    shared = per_peer * chips
    firsts = [sum(SIZES[:g]) for g in range(GROUPS)]
    parts = [(2 * per_peer * 4 * size + 15) // 16 * 16 for size in SIZES]
    me = lax.axis_index("dp")
    chip = me // 2
    core = lax.rem(me, 2)
    sibling = {"dp": 2 * chip + 1 - core}
    count = lax.axis_size("seq")
    block = lax.axis_index("seq")
    right = {"seq": lax.rem(block + 1, count)}
    left = {"seq": lax.rem(block + count - 1, count)}

    loads = [
        pltpu.make_async_copy(ref, loaded.at[a], load_sems.at[a])
        for a, ref in enumerate((query_ref, key_ref, value_ref, grad_ref))
    ]
    for c in loads:
        c.start()

    barrier = pltpu.get_barrier_semaphore()
    for neighbour in (left, right):
        pl.semaphore_signal(barrier, inc=1, device_id=neighbour, device_id_type=MESH)

    def greet(i, carry):
        pl.semaphore_signal(barrier, inc=1, device_id={"dp": lax.rem(me + i, peers)}, device_id_type=MESH)
        return carry

    lax.fori_loop(1, peers, greet, 0)

    def copy(src, dst, sems, which, h, target):
        return pltpu.make_async_remote_copy(
            src_ref=src,
            dst_ref=dst,
            send_sem=sems.at[0, which, h],
            recv_sem=sems.at[1, which, h],
            device_id=target,
            device_id_type=MESH,
        )

    def near_copies(h):
        return (
            copy(keys.at[h, :, pl.ds(2 * rows, rows)], keys.at[h, :, pl.ds(rows, rows)], in_sems, 0, h, right),
            copy(queries.at[h, :, pl.ds(0, rows)], queries.at[h, :, pl.ds(rows, rows)], in_sems, 1, h, left),
        )

    def far_copies(h):
        return (
            copy(keys.at[h, :, pl.ds(rows, rows)], keys.at[h, :, pl.ds(0, rows)], in_sems, 2, h, right),
            copy(queries.at[h, :, pl.ds(rows, rows)], queries.at[h, :, pl.ds(2 * rows, rows)], in_sems, 3, h, left),
        )

    def far_returns(h):
        return (
            copy(far_out.at[h, 0], far_in.at[h, 0], out_sems, 0, h, right),
            copy(far_out.at[h, 1], far_in.at[h, 1], out_sems, 1, h, left),
        )

    def near_returns(h):
        return (
            copy(near_out.at[h, 0], near_in.at[h, 0], out_sems, 2, h, right),
            copy(near_out.at[h, 1], near_in.at[h, 1], out_sems, 3, h, left),
        )

    def send_group(source, target, g, which):
        part = parts[g]

        def send(i, carry):
            other = lax.rem(chip + i, chips)
            source[g, other, pl.ds(0, part), :] = mixed[pl.ds(pl.multiple_of(other * part, 16), part), :].astype(jnp.bfloat16)
            piece, place_there = source.at[g, other, pl.ds(0, part)], target.at[g, chip, pl.ds(0, part)]
            copy(piece, place_there, all_sems, which, g, {"dp": 2 * other + core}).start()
            return carry

        lax.fori_loop(1, chips, send, 0)
        target[g, chip, pl.ds(0, part), :] = mixed[pl.ds(pl.multiple_of(chip * part, 16), part), :].astype(jnp.bfloat16)

    def wait_all(ref, side, which, g):
        whole = ref.at[g, pl.ds(0, chips - 1), pl.ds(0, parts[g])]
        pltpu.make_async_copy(whole, whole, all_sems.at[side, which, g]).wait()

    def hand_copy(source, target, g, which):
        used = pl.ds(0, 4 * SIZES[g])
        return copy(source.at[g, used], target.at[g, used, pl.ds(shared, shared)], all_sems, which, g, sibling)

    def hand_over(source, given, target, g, which):
        wait_all(source, 1, which, g)
        part, chunks = parts[g], 4 * SIZES[g]
        came_rows = source[g, :, pl.ds(0, part), :].reshape(chips * part, HDIM)
        mixed[pl.ds(0, chips * part), :] = came_rows.astype(jnp.float32)
        for c in range(chunks):
            for t in range(per_peer):
                first = mixed[pl.ds(t * chunks + c, chips, stride=part), :]
                second = mixed[pl.ds((per_peer + t) * chunks + c, chips, stride=part), :]
                given[g, c, pl.ds(t * chips, chips), :] = jnp.where(core == 0, second, first).astype(jnp.bfloat16)
        hand_copy(given, target, g, which + 3).start()
        for c in range(chunks):
            for t in range(per_peer):
                first = mixed[pl.ds(t * chunks + c, chips, stride=part), :]
                second = mixed[pl.ds((per_peer + t) * chunks + c, chips, stride=part), :]
                target[g, c, pl.ds(t * chips, chips), :] = jnp.where(core == 0, first, second).astype(jnp.bfloat16)

    targets = dest_ref[...].astype(jnp.float32)
    across = jnp.broadcast_to(targets, (rows, rows))
    ranks = jnp.sum(jnp.where(across.T < across, jnp.float32(1.0), jnp.float32(0.0)), axis=0, keepdims=True)
    steps = lax.broadcasted_iota(jnp.int32, (rows, rows), 0).astype(jnp.float32)
    holder = jnp.floor((ranks + 0.5) * (1.0 / per_peer))
    holder_chip = jnp.floor((holder + 0.5) * 0.5)
    mailed = (ranks - holder_chip * (2 * per_peer)) * chips + holder_chip
    order = jnp.where(steps == mailed, jnp.float32(1.0), jnp.float32(0.0)).astype(jnp.bfloat16)
    away = jnp.abs(holder - 2.0 * holder_chip - core.astype(jnp.float32))
    spots = away * shared + (ranks - holder * per_peer) * chips + holder_chip
    restore = jnp.where(steps == spots, jnp.float32(1.0), jnp.float32(0.0)).T.astype(jnp.bfloat16)

    mixed[...] = jnp.zeros_like(mixed)

    def mix(g, c, values):
        for u in range(2 * per_peer):
            mixed[pl.ds(u * 4 * SIZES[g] + c, chips, stride=parts[g]), :] = values[u * chips : (u + 1) * chips]

    def pack_group(g):
        for a in range(4):
            sorted_rows = dot_nn(order, loaded[a, :, pl.ds(firsts[g] * HDIM, SIZES[g] * HDIM)])
            for i in range(SIZES[g]):
                mix(g, 4 * i + a, sorted_rows[:, i * HDIM : (i + 1) * HDIM])
        if g == 0:
            pl.semaphore_wait(barrier, peers + 1)
        send_group(packed, arrived, g, 0)

    width = slots_out.shape[2]
    lane = lax.broadcasted_iota(jnp.int32, (peers, 1, width), 2)
    receiver = lax.broadcasted_iota(jnp.int32, (peers, 1, 1), 0)
    apart = jnp.where(lax.rem(receiver, 2) == core, 0, shared)
    slots = jnp.zeros((peers, 1, width), jnp.float32)
    base = (receiver * rows).astype(jnp.float32)
    first_rank = (receiver * per_peer).astype(jnp.float32)
    for t in range(per_peer):
        hit = ranks.reshape(1, 1, rows) == first_rank + t
        slot = jnp.sum(jnp.where(hit, targets.reshape(1, 1, rows), jnp.float32(0.0)), axis=2, keepdims=True) - base
        slots = jnp.where(lane == apart + t * chips + chip, slot, slots)
        slots = jnp.where(lane == width // 2 + (core * per_peer + t) * chips + chip, slot, slots)
    slots_out[...] = slots

    for c in loads:
        c.wait()
    pack_group(0)
    def send_slots(i, carry):
        peer = lax.rem(me + i, peers)
        copy(slots_out.at[peer], slots_in.at[me], all_sems, 2, 0, {"dp": peer}).start()
        return carry

    lax.fori_loop(1, peers, send_slots, 0)
    slots_in[me] = slots_out[me]

    for g in range(1, GROUPS):
        pack_group(g)

    weight = jnp.float32(1.0 / (REACH * rows))
    first = block * rows
    for ref, query_first, key_first in (
        (weight_own, first, first - rows),
        (weight_near, first + rows, first - 2 * rows),
        (weight_far, first + 2 * rows, first - 2 * rows),
    ):
        mask = pair_weight(lengths_ref, query_first, ref.shape[0], key_first, ref.shape[1])
        ref[...] = jnp.where(mask, weight, jnp.float32(0.0))

    everyone = slots_in.at[pl.ds(0, peers - 1)]
    pltpu.make_async_copy(everyone, everyone, all_sems.at[1, 2, 0]).wait()
    slot_row = jnp.sum(slots_in[...], axis=0)
    place = jnp.where(steps == slot_row[:, :rows], jnp.float32(1.0), jnp.float32(0.0)).astype(jnp.bfloat16)
    back = slot_row[:, width // 2 : width // 2 + rows]
    unplace = jnp.where(steps == back, jnp.float32(1.0), jnp.float32(0.0)).T.astype(jnp.bfloat16)

    def each_head(g, step):
        def run(h, carry):
            step(h)
            return carry

        lax.fori_loop(firsts[g], firsts[g] + SIZES[g], run, 0)

    def unpack(g):
        hand_over(arrived, handed, came, g, 0)

    def place_group(g):
        hand_copy(handed, came, g, 3).wait_recv()
        for i in range(SIZES[g]):
            h = firsts[g] + i
            for a, (buffer, k, start) in enumerate(
                ((queries, 0, 0), (keys, 0, 2 * rows), (keys, 1, 2 * rows), (queries, 1, 0))
            ):
                buffer[h, k, pl.ds(start, rows), :] = dot_nn(place, came[g, 4 * i + a]).astype(jnp.bfloat16)
            for c in near_copies(h):
                c.start()

    def forward(h):
        for c in near_copies(h):
            c.wait_recv()
        for c in far_copies(h):
            c.start()

    def compute(h):
        for c in far_copies(h):
            c.wait_recv()
        key, value = keys[h, 0], keys[h, 1]
        query, grad = queries[h, 0], queries[h, 1]
        far = pair_terms(query[2 * rows :], grad[2 * rows :], key[:rows], value[:rows], weight_far[...])
        near = pair_terms(
            query[rows : 2 * rows], grad[rows : 2 * rows], key[: 2 * rows], value[: 2 * rows], weight_near[...]
        )
        far_out[h, 0, 0] = far[0].astype(jnp.bfloat16)
        far_out[h, 0, 1] = far[1].astype(jnp.bfloat16)
        far_out[h, 1, 0] = (far[2] + near[2][:rows]).astype(jnp.bfloat16)
        far_out[h, 1, 1] = (far[3] + near[3][:rows]).astype(jnp.bfloat16)
        for c in far_returns(h):
            c.start()
        own = pair_terms(query[:rows], grad[:rows], key[rows:], value[rows:], weight_own[...])
        near_sum[h, 0, 0] = near[0]
        near_sum[h, 0, 1] = near[1]
        near_sum[h, 1, 0] = near[2][rows:] + own[2][:rows]
        near_sum[h, 1, 1] = near[3][rows:] + own[3][:rows]
        own_sum[h, 0, 0] = own[0]
        own_sum[h, 0, 1] = own[1]
        own_sum[h, 1, 0] = own[2][rows:]
        own_sum[h, 1, 1] = own[3][rows:]

    def relay(h):
        for c in far_returns(h):
            c.wait_recv()
        near_out[h] = (near_sum[h] + far_in[h].astype(jnp.float32)).astype(jnp.bfloat16)
        for c in near_returns(h):
            c.start()

    def finish(g):
        for i in range(SIZES[g]):
            h = firsts[g] + i
            for c in near_returns(h):
                c.wait_recv()
            for side in range(2):
                for k in range(2):
                    total = (own_sum[h, side, k] + near_in[h, side, k].astype(jnp.float32)).astype(jnp.bfloat16)
                    mix(g, 4 * i + 2 * side + k, dot_nn(unplace, total))
        send_group(packed_back, arrived_back, g, 1)

    def unpack_back(g):
        hand_over(arrived_back, handed_back, came_back, g, 1)

    def restore_group(g):
        hand_copy(handed_back, came_back, g, 4).wait_recv()
        for i in range(SIZES[g]):
            lanes = pl.ds((firsts[g] + i) * HDIM, HDIM)
            for a, ref in enumerate((out_ref, grad_query_ref, grad_key_ref, grad_value_ref)):
                ref[:, lanes] = dot_nn(restore, came_back[g, 4 * i + a]).astype(jnp.bfloat16)

    unpack(0)
    place_group(0)
    each_head(0, forward)
    unpack(1)
    for g in range(1, GROUPS):
        place_group(g)
        each_head(g - 1, compute)
        if g > 1:
            finish(g - 2)
        each_head(g, forward)
        if g + 1 < GROUPS:
            unpack(g + 1)
        each_head(g - 1, relay)
    each_head(GROUPS - 1, compute)
    finish(GROUPS - 2)
    each_head(GROUPS - 1, relay)
    finish(GROUPS - 1)
    for g in range(GROUPS - 1):
        unpack_back(g)
    for g in range(GROUPS - 1):
        restore_group(g)

    def settle(h):
        for c in near_copies(h) + far_copies(h) + far_returns(h) + near_returns(h):
            c.wait_send()

    for g in range(GROUPS):
        each_head(g, settle)
        wait_all(packed, 0, 0, g)
        hand_copy(handed, came, g, 3).wait_send()
    pltpu.make_async_copy(everyone, everyone, all_sems.at[0, 2, 0]).wait()
    unpack_back(GROUPS - 1)
    restore_group(GROUPS - 1)
    for g in range(GROUPS):
        wait_all(packed_back, 0, 1, g)
        hand_copy(handed_back, came_back, g, 4).wait_send()


def shards(queries, keys, values, grad_out, dest, lengths):
    _, rows, width = queries.shape
    heads = width // HDIM
    peers = lax.axis_size("dp")
    chunks = 4 * max(SIZES)
    part = rows // peers * 2 * chunks
    blocks = lambda *lead: pltpu.VMEM((heads,) + lead + (HDIM,), jnp.bfloat16)
    totals = pltpu.VMEM((heads, 2, 2, rows, HDIM), jnp.float32)
    pieces = pltpu.VMEM((GROUPS, peers // 2, part, HDIM), jnp.bfloat16)
    handed = pltpu.VMEM((GROUPS, chunks, rows // 2, HDIM), jnp.bfloat16)
    came = pltpu.VMEM((GROUPS, chunks, rows, HDIM), jnp.bfloat16)
    slots = pltpu.VMEM((peers, 1, (rows + 127) // 128 * 256), jnp.float32)
    vmem = pl.BlockSpec(memory_space=pltpu.VMEM)
    results = pl.pallas_call(
        whole_kernel,
        out_shape=[jax.ShapeDtypeStruct((rows, width), jnp.bfloat16)] * 4,
        in_specs=[pl.BlockSpec(memory_space=pltpu.SMEM), vmem] + [pl.BlockSpec(memory_space=pltpu.HBM)] * 4,
        out_specs=[vmem] * 4,
        scratch_shapes=[
            pltpu.VMEM((4, rows, width), jnp.bfloat16),
            pltpu.VMEM((peers // 2 * part, HDIM), jnp.float32),
            pieces,
            pieces,
            pieces,
            pieces,
            handed,
            came,
            handed,
            came,
            slots,
            slots,
            blocks(2, 3 * rows),
            blocks(2, 3 * rows),
            blocks(2, 2, rows),
            blocks(2, 2, rows),
            blocks(2, 2, rows),
            blocks(2, 2, rows),
            totals,
            totals,
            pltpu.VMEM((rows, 2 * rows), jnp.float32),
            pltpu.VMEM((rows, 2 * rows), jnp.float32),
            pltpu.VMEM((rows, rows), jnp.float32),
            pltpu.SemaphoreType.DMA((2, 4, heads)),
            pltpu.SemaphoreType.DMA((2, 4, heads)),
            pltpu.SemaphoreType.DMA((2, 5, GROUPS)),
            pltpu.SemaphoreType.DMA((4,)),
        ],
        compiler_params=pltpu.CompilerParams(
            collective_id=0, has_side_effects=True, vmem_limit_bytes=52 * 1024 * 1024
        ),
        name="whole",
    )(lengths, dest, queries[0], keys[0], values[0], grad_out[0])
    return tuple(result[None] for result in results)


def solution(mesh):
    rows = P("seq", "dp", None)
    return jax.shard_map(
        shards,
        mesh=mesh,
        in_specs=(rows, rows, rows, rows, P("seq", "dp"), P("dp", None)),
        out_specs=(rows, rows, rows, rows),
        check_vma=False,
    )
```
